32 devices in a mesh: dp: 8 (over z, x), rows: 4 (over y, core).
Axes of the slice: x: 2, y: 2, z: 4, core: 2. Of those that a mesh axis runs over, the one named last changes fastest.
Arguments:
- activations: bfloat16 [16384, 8192], P('dp', 'rows'), may hold values from -6 to 6
- key_grads: bfloat16 [16384, 1024], P('dp'), may hold values from -0.125 to 0.125
- momentum: float32 [8, 8192, 1024], P('dp', 'rows'), may hold values from -6 to 6
- basis: float32 [1024, 128], replicated, may hold values from -0.1875 to 0.1875
Outputs:
- new_momentum: float32 [8, 8192, 1024], P('dp', 'rows')
- new_basis: float32 [1024, 128], P('rows')
- update: bfloat16 [8192, 1024], P(('rows', 'dp'))
The draws below stay inside these ranges and needn't reach their ends.
All inputs are finite; a program needn't handle non-finite values.
Results may differ from the reference program's by a relative error of at most 0.0015.
Values sent between devices are 32-bit elements; how exact they have to be, the bound alone decides.
No kernel may reach another device: no remote copies, remote signals or barrier semaphores. Data moves between devices by JAX's collectives and lax.ppermute only.
A program may use at most 64 MiB of HBM per device.

```python
import math
import jax
import jax.numpy as jnp
from jax import lax

D = 8192
KV = 1024
RANK = 128
TOK_DEV = 2048
TOKENS = 16384
REPLICAS = 8
N_DP = 8


def levels(rng, extent, split, low, high):
    gain = 1.0
    for position, parts in split:
        heights = jax.random.uniform(jax.random.fold_in(jax.random.fold_in(rng, 6), position), (parts,), jnp.float32, low / len(split), high / len(split))
        gain = gain * jnp.repeat(jnp.exp(heights), extent[position] // parts).reshape((-1,) + (1,) * (len(extent) - 1 - position))
    return gain


def bell_draw(own_key, shape, deviation, most, shards=(), kind=jnp.bfloat16):
    result = jax.random.normal(own_key, shape, jnp.float32) * deviation
    if len(shards) > 0:
        result = levels(own_key, shape, shards, -0.22, 0.18) * result
    return jnp.clip(result, min=-most, max=most).astype(kind)


def setup_inputs(seed: int = 0) -> dict:
    streams_of = jax.random.split(jax.random.key(seed), 5)
    activations = bell_draw(streams_of[0], (TOKENS, D), 1.0, 6.0, ((0, 8), (1, 4)))
    key_grads = bell_draw(streams_of[1], (TOKENS, KV), TOK_DEV ** -0.5, 0.125, ((0, 8),))
    momentum = bell_draw(streams_of[2], (REPLICAS, D, KV), 1.0, 6.0, ((0, 8), (1, 4)), jnp.float32)
    basis = bell_draw(streams_of[3], (KV, RANK), KV ** -0.5, 0.1875, (), jnp.float32)
    return dict(activations=activations, key_grads=key_grads, momentum=momentum, basis=basis)


def reference(activations, key_grads, momentum, basis):
    high = lax.Precision.HIGHEST
    acts = activations.reshape(N_DP, TOK_DEV, D)
    grads = key_grads.reshape(N_DP, TOK_DEV, KV)

    def one_grad(pair):
        return lax.dot_general(pair[0].astype(jnp.float32), pair[1].astype(jnp.float32), (((0,), (0,)), ((), ())), preferred_element_type=jnp.float32)
    blended = momentum + lax.map(one_grad, (acts, grads))
    sketch = jnp.einsum('ide,er->dr', blended, basis, precision=high) / N_DP
    gram = jnp.dot(sketch.T, sketch, precision=high)
    lower = jnp.linalg.cholesky(gram)
    ortho = lax.linalg.triangular_solve(lower, sketch, left_side=False, lower=True, transpose_a=True)
    coeff = jnp.einsum('ide,dr->er', blended, ortho, precision=high) / N_DP
    feedback = jnp.dot(ortho, coeff.T, precision=high)
    new_momentum = blended - 0.2 * feedback[None]
    col_norm = jnp.sqrt(lax.optimization_barrier(jnp.sum(coeff * coeff, axis=0)) + 1e-06)
    new_basis = coeff / col_norm
    update = math.sqrt(D * KV / RANK) * jnp.dot(ortho, new_basis.T, precision=high)
    return (new_momentum, new_basis, update.astype(jnp.bfloat16))
```

```python
import math

import jax
import jax.numpy as jnp
from jax import lax
from jax.sharding import PartitionSpec as P

HIGH = lax.Precision.HIGH
HIGHEST = lax.Precision.HIGHEST


def swap(value, axis, mask):
    count = lax.axis_size(axis)
    return lax.ppermute(value, axis, [(i, i ^ mask) for i in range(count)])


def bits_of(count):
    return [1 << b for b in range(count.bit_length() - 1)]


def halve(value, axis, mask):
    half = value.shape[0] // 2
    bit = jnp.where((lax.axis_index(axis) & mask) != 0, 1, 0)
    keep = lax.dynamic_slice_in_dim(value, bit * half, half, 0)
    give = lax.dynamic_slice_in_dim(value, (1 - bit) * half, half, 0)
    return keep + swap(give, axis, mask)


def double(value, axis, mask):
    other = swap(value, axis, mask)
    mine_first = (lax.axis_index(axis) & mask) == 0
    return jnp.concatenate([jnp.where(mine_first, value, other), jnp.where(mine_first, other, value)], 0)


def body(activations, key_grads, momentum, basis):
    n_dp = lax.axis_size("dp")
    n_rows = lax.axis_size("rows")
    dp = lax.axis_index("dp")
    grad = lax.dot_general(
        activations, key_grads, (((0,), (0,)), ((), ())), preferred_element_type=jnp.float32
    )
    blended = momentum[0] + grad
    local_rows = blended.shape[0]
    kv = blended.shape[1]
    rank = basis.shape[1]
    sketch = jnp.dot(blended, basis, precision=HIGH)

    group = min(4, n_dp)
    low = dp & (group - 1)
    block = local_rows // group
    parts = [lax.dynamic_slice_in_dim(sketch, (low ^ s) * block, block, 0) for s in range(group)]
    own = parts[0]
    for s in range(group - 1, 0, -1):
        own = own + swap(parts[s], "dp", s)
    for mask in bits_of(n_dp):
        if mask >= group:
            own = own + swap(own, "dp", mask)
    own = own / n_dp
    total = jnp.zeros((local_rows, rank), jnp.float32)
    total = lax.dynamic_update_slice_in_dim(total, own, low * block, 0)
    for s in range(group - 1, 0, -1):
        total = lax.dynamic_update_slice_in_dim(total, swap(own, "dp", s), (low ^ s) * block, 0)

    right = lax.dot_general(
        blended, total, (((0,), (0,)), ((), ())), precision=HIGH, preferred_element_type=jnp.float32
    ) / n_dp
    gram = lax.dot_general(
        own, own, (((0,), (0,)), ((), ())), precision=HIGHEST, preferred_element_type=jnp.float32
    ) * (group / n_dp)
    both = jnp.concatenate([right, gram], 0)
    steps = [("rows", m) for m in bits_of(n_rows)] + [("dp", 1)]
    for axis, mask in steps:
        both = halve(both, axis, mask)
    for mask in bits_of(n_dp)[1:]:
        both = both + swap(both, "dp", mask)
    for axis, mask in steps[::-1]:
        both = double(both, axis, mask)
    right, gram = both[:kv], both[kv:]

    lower = jnp.linalg.cholesky(gram)
    inverse = lax.linalg.triangular_solve(lower, jnp.eye(rank, dtype=jnp.float32), left_side=True, lower=True)
    coeff = lax.dot_general(right, inverse, (((1,), (1,)), ((), ())), precision=HIGHEST)
    middle = jnp.dot(coeff, inverse, precision=HIGHEST)
    feedback = lax.dot_general(
        total, middle, (((1,), (1,)), ((), ())), precision=HIGH, preferred_element_type=jnp.float32
    )
    new_momentum = (blended - 0.2 * feedback)[None]
    col_norm = jnp.sqrt(jnp.sum(coeff * coeff, axis=0) + 1e-06)
    normed = coeff / col_norm
    basis_rows = kv // n_rows
    new_basis = lax.dynamic_slice_in_dim(normed, lax.axis_index("rows") * basis_rows, basis_rows, 0)
    own_count = local_rows // n_dp
    own_rows = lax.dynamic_slice_in_dim(total, dp * own_count, own_count, 0)
    own_ortho = lax.dot_general(own_rows, inverse, (((1,), (1,)), ((), ())), precision=HIGHEST)
    scale = math.sqrt(local_rows * n_rows * kv / rank)
    update = scale * lax.dot_general(
        own_ortho, normed, (((1,), (1,)), ((), ())), precision=HIGHEST, preferred_element_type=jnp.float32
    )
    return (new_momentum, new_basis, update.astype(jnp.bfloat16))


def solution(mesh):
    in_specs = (P("dp", "rows"), P("dp", None), P("dp", "rows", None), P())
    out_specs = (P("dp", "rows", None), P("rows", None), P(("rows", "dp"), None))
    return jax.shard_map(body, mesh=mesh, in_specs=in_specs, out_specs=out_specs, check_vma=False)
```

```python
import functools
import math

import jax
import jax.numpy as jnp
from jax import lax
from jax.experimental import pallas as pl
from jax.experimental.pallas import tpu as pltpu
from jax.sharding import PartitionSpec as P

VMEM_LIMIT = 60 * 1024 * 1024
EXACT = lax.Precision.HIGHEST


def split(value):
    high = value.astype(jnp.bfloat16)
    return high, (value - high.astype(jnp.float32)).astype(jnp.bfloat16)


def dot(left, right, left_dim, right_dim, precision=None):
    return lax.dot_general(
        left,
        right,
        (((left_dim,), (right_dim,)), ((), ())),
        precision=precision,
        preferred_element_type=jnp.float32,
    )


def params(**more):
    return pltpu.CompilerParams(vmem_limit_bytes=VMEM_LIMIT, **more)


def swap(value, masks):
    axes = tuple(a for a in ("dp", "rows") if a in masks)
    sizes = [lax.axis_size(a) for a in axes]
    pairs = []
    for index in range(math.prod(sizes)):
        rest, there = index, 0
        coords = []
        for size in sizes[::-1]:
            coords.append(rest % size)
            rest //= size
        for axis, size, coord in zip(axes, sizes, coords[::-1]):
            there = there * size + (coord ^ masks[axis])
        pairs.append((index, there))
    return lax.ppermute(value, axes, pairs)


def bits_of(count):
    return [1 << b for b in range(count.bit_length() - 1)]


def bit_set(axis, mask):
    return jnp.where((lax.axis_index(axis) & mask) != 0, 1, 0).astype(jnp.int32)


def masks_of(chosen):
    masks = {}
    for axis, mask in chosen:
        masks[axis] = masks.get(axis, 0) | mask
    return masks


def scatter_sum(value, directions):
    count = 1 << len(directions)
    block = value.shape[0] // count
    mine = sum(bit_set(a, m) << b for b, (a, m) in enumerate(directions))
    parts = []
    for s in range(count - 1, 0, -1):
        give = lax.dynamic_slice_in_dim(value, (mine ^ s) * block, block, 0)
        parts.append(swap(give, masks_of([d for b, d in enumerate(directions) if s >> b & 1])))
    total = lax.dynamic_slice_in_dim(value, mine * block, block, 0)
    for part in parts:
        total = total + part
    return total


def gather(value, directions):
    count = 1 << len(directions)
    block = value.shape[0]
    mine = sum(bit_set(a, m) << b for b, (a, m) in enumerate(directions))
    parts = [value] + [
        swap(value, masks_of([d for b, d in enumerate(directions) if s >> b & 1])) for s in range(1, count)
    ]
    out = jnp.zeros((count * block,) + value.shape[1:], value.dtype)
    for s, part in enumerate(parts):
        out = lax.dynamic_update_slice_in_dim(out, part, (mine ^ s) * block, 0)
    return out


def blend_kernel(count, chained, who, acts, grads, momentum, basis, *refs):
    refs = refs[1:] if chained else refs
    blended, sketches = refs[0], refs[1:]
    rank = basis.shape[1]
    basis_high, basis_low = split(basis[...])
    both = jnp.concatenate([basis_high, basis_low], 1)
    rows = blended.shape[0]
    part = rows // 2
    outs = []
    for first in range(0, rows, part):
        here = pl.ds(first, part)
        value = momentum[here, :] + dot(acts[:, here], grads[...], 0, 0)
        blended[here, :] = value
        high, low = split(value)
        wide = dot(high, both, 1, 0)
        outs.append(wide[:, :rank] + wide[:, rank:] + dot(low, basis_high, 1, 0))
    result = jnp.concatenate(outs, 0)
    if count == 1:
        sketches[0][...] = result
    else:
        step = pl.program_id(0)
        for index, sketch in enumerate(sketches):

            @pl.when(step == index)
            def _(sketch=sketch):
                sketch[...] = result


def blend(low, acts, grads, momentum, basis, group, first, count, chain=None):
    tokens, rows = acts.shape
    kv, rank = basis.shape
    block = rows // group

    def where(i, who):
        return who[0] ^ (first - i)

    in_specs = [
        pl.BlockSpec((tokens, block), lambda i, who: (0, where(i, who))),
        pl.BlockSpec((tokens, kv), lambda i, who: (0, 0), pipeline_mode=pl.Buffered(1)),
        pl.BlockSpec((block, kv), lambda i, who: (where(i, who), 0)),
        pl.BlockSpec((kv, rank), lambda i, who: (0, 0), pipeline_mode=pl.Buffered(1)),
    ]
    operands = [low, acts, grads, momentum, basis]
    aliases = {}
    if chain is not None:
        in_specs.append(pl.BlockSpec(memory_space=pl.ANY))
        aliases = {len(operands): 0}
        operands.append(chain)
    out = pl.pallas_call(
        functools.partial(blend_kernel, count, chain is not None),
        grid_spec=pltpu.PrefetchScalarGridSpec(
            num_scalar_prefetch=1,
            grid=(count,),
            in_specs=in_specs,
            out_specs=[pl.BlockSpec((block, kv), lambda i, who: (where(i, who), 0))]
            + [pl.BlockSpec((block, rank), lambda i, who: (0, 0))] * count,
        ),
        out_shape=[jax.ShapeDtypeStruct((rows, kv), jnp.float32)]
        + [jax.ShapeDtypeStruct((block, rank), jnp.float32)] * count,
        input_output_aliases=aliases,
        compiler_params=params(),
        cost_estimate=pl.CostEstimate(
            flops=2 * count * block * tokens * kv, bytes_accessed=4 * count * block * kv * 3, transcendentals=0
        ),
        name="blend",
    )(*operands)
    return out[0], out[1:]


def right_product(sketch, blended):
    high, low = split(sketch.T)
    blended_high, blended_low = split(blended)
    rank = high.shape[0]
    wide = dot(jnp.concatenate([high, low], 0), blended_high, 1, 0)
    return wide[:rank] + wide[rank:] + dot(high, blended_low, 1, 0)


def right_first_kernel(share, scale, who, sketch, blended, right):
    value = sketch[...]
    right[:, : blended.shape[1]] = scale * right_product(value, blended[...])
    right[:, blended.shape[1] :] = share * dot(value, value, 0, 0, EXACT)


def right_next_kernel(scale, who, sketch, blended, before, right):
    kv = blended.shape[1]
    right[:, :kv] = before[:, :kv] + scale * right_product(sketch[...], blended[...])
    right[:, kv:] = before[:, kv:]


def right_term(low, sketch, blended, offset, scale, share, before=None):
    block, rank = sketch.shape
    kv = blended.shape[1]
    in_specs = [
        pl.BlockSpec((block, rank), lambda i, who: (0, 0)),
        pl.BlockSpec((block, kv), lambda i, who: (who[0] ^ offset, 0)),
    ]
    operands = [low, sketch, blended]
    whole = pl.BlockSpec((rank, kv + rank), lambda i, who: (0, 0))
    if before is None:
        kernel = functools.partial(right_first_kernel, share, scale)
    else:
        kernel = functools.partial(right_next_kernel, scale)
        in_specs.append(whole)
        operands.append(before)
    return pl.pallas_call(
        kernel,
        grid_spec=pltpu.PrefetchScalarGridSpec(
            num_scalar_prefetch=1, grid=(1,), in_specs=in_specs, out_specs=whole
        ),
        out_shape=jax.ShapeDtypeStruct((rank, kv + rank), jnp.float32),
        compiler_params=params(),
        cost_estimate=pl.CostEstimate(
            flops=6 * block * rank * kv, bytes_accessed=4 * block * kv, transcendentals=0
        ),
        name="right_term",
    )(*operands)


def factor_kernel(gram, inverse, work):
    rank = gram.shape[0]
    rows_id = lax.broadcasted_iota(jnp.int32, (rank, rank), 0)
    cols_id = lax.broadcasted_iota(jnp.int32, (rank, rank), 1)
    work[:, :rank] = gram[...]
    work[:, rank:] = jnp.where(rows_id == cols_id, 1.0, 0.0)
    panel = 16
    for start in range(0, rank, panel):
        here = slice(start, start + panel)
        rows = work[here, :]
        index = lax.broadcasted_iota(jnp.int32, (panel, 1), 0)
        for j in range(0, panel, 2):
            col_a = rows[:, start + j : start + j + 1]
            col_b = rows[:, start + j + 1 : start + j + 2]
            row_a = rows[j : j + 1, :]
            row_b = rows[j + 1 : j + 2, :]
            p_aa = col_a[j : j + 1, :]
            p_ab = col_b[j : j + 1, :]
            p_bb = col_b[j + 1 : j + 2, :]
            inv_a = 1.0 / p_aa
            ratio = p_ab * inv_a
            inv_b = 1.0 / (p_bb - ratio * p_ab)
            row_b = row_b - ratio * row_a
            col_b = col_b - ratio * col_a
            scale_a = jnp.where(index > j, col_a * inv_a, 0.0)
            scale_b = jnp.where(index > j + 1, col_b * inv_b, 0.0)
            rows = rows - scale_a * row_a - scale_b * row_b
        diagonal = jnp.sum(
            jnp.where(
                lax.broadcasted_iota(jnp.int32, (panel, panel), 0)
                == lax.broadcasted_iota(jnp.int32, (panel, panel), 1),
                rows[:, start : start + panel],
                0.0,
            ),
            axis=1,
            keepdims=True,
        )
        rows = rows / jnp.sqrt(diagonal)
        work[here, :] = rows
        if start + panel < rank:
            below = slice(start + panel, rank)
            left = rows[:, :rank]
            update = dot(left, rows, 0, 0, EXACT)
            work[below, :] = work[below, :] - update[start + panel :, :]
    inverse[...] = work[:, rank:]


def factor(gram):
    rank = gram.shape[0]
    return pl.pallas_call(
        factor_kernel,
        out_shape=jax.ShapeDtypeStruct((rank, rank), jnp.float32),
        scratch_shapes=[pltpu.VMEM((rank, 2 * rank), jnp.float32)],
        compiler_params=params(),
        name="factor",
    )(gram)


def finish_kernel(group, scale, who, right, inverse, blended, *refs):
    sketches = refs[:group]
    new_momentum, new_basis, update, total, middle_high, middle_low = refs[group:]
    step = pl.program_id(0)
    block = sketches[0].shape[0]

    @pl.when(step == 0)
    def _():
        for s in range(group):
            total[pl.ds(pl.multiple_of((who[0] ^ s) * block, block), block), :] = sketches[s][...]
        kv = right.shape[1]
        rank = right.shape[0]
        factor_inverse = inverse[...]
        coeff = dot(factor_inverse, right[...], 1, 0, EXACT)
        middle = dot(factor_inverse, coeff, 0, 0, EXACT)
        high, low = split(0.2 * middle)
        middle_high[...] = high
        middle_low[...] = low
        norm = jnp.sqrt(jnp.sum(coeff * coeff, axis=1, keepdims=True) + 1e-06)
        normed = coeff / norm
        count = new_basis.shape[0]
        for j in range(kv // count):

            @pl.when(who[2] == j)
            def _(j=j):
                new_basis[...] = normed[:, j * count : (j + 1) * count].T

        own = update.shape[0]
        own_rows = total[pl.ds(pl.multiple_of(who[1] * own, own), own), :]
        ortho = dot(own_rows, factor_inverse, 1, 1, EXACT)
        update[...] = (scale * dot(ortho, normed, 1, 0, EXACT)).astype(update.dtype)

    here = pl.ds(pl.multiple_of(step * block, block), block)
    high, low = split(total[here, :])
    feedback = dot(jnp.concatenate([high, low], 1), jnp.concatenate([middle_high[...], middle_high[...]], 0), 1, 0)
    feedback = feedback + dot(high, middle_low[...], 1, 0)
    new_momentum[...] = blended[...] - feedback


def finish(who, right, inverse, blended, sketches, n_dp, n_rows, scale):
    rows, kv = blended.shape
    rank = inverse.shape[0]
    group = len(sketches)
    block = rows // group
    const = lambda i, who: (0, 0)
    return pl.pallas_call(
        functools.partial(finish_kernel, group, scale),
        grid_spec=pltpu.PrefetchScalarGridSpec(
            num_scalar_prefetch=1,
            grid=(group,),
            in_specs=[
                pl.BlockSpec((rank, kv), const),
                pl.BlockSpec((rank, rank), const),
                pl.BlockSpec((block, kv), lambda i, who: (i, 0)),
            ]
            + [pl.BlockSpec((block, rank), const)] * group,
            out_specs=[
                pl.BlockSpec((block, kv), lambda i, who: (i, 0)),
                pl.BlockSpec((kv // n_rows, rank), const),
                pl.BlockSpec((rows // n_dp, kv), const),
            ],
            scratch_shapes=[
                pltpu.VMEM((rows, rank), jnp.float32),
                pltpu.VMEM((rank, kv), jnp.bfloat16),
                pltpu.VMEM((rank, kv), jnp.bfloat16),
            ],
        ),
        out_shape=[
            jax.ShapeDtypeStruct((rows, kv), jnp.float32),
            jax.ShapeDtypeStruct((kv // n_rows, rank), jnp.float32),
            jax.ShapeDtypeStruct((rows // n_dp, kv), jnp.bfloat16),
        ],
        compiler_params=params(),
        name="finish",
    )(who, right, inverse, blended, *sketches)


def body(activations, key_grads, momentum, basis):
    n_dp = lax.axis_size("dp")
    n_rows = lax.axis_size("rows")
    dp = lax.axis_index("dp")
    group = min(4, n_dp)
    low = dp & (group - 1)
    who = jnp.stack([low, dp, lax.axis_index("rows")]).astype(jnp.int32)
    kv, rank = basis.shape
    local_rows = activations.shape[1]

    blended, others = blend(who, activations, key_grads, momentum[0], basis, group, group - 1, group - 1)
    arrived = [swap(sketch, {"dp": group - 1 - i}) for i, sketch in enumerate(others)]
    blended, (own,) = blend(who, activations, key_grads, momentum[0], basis, group, 0, 1, blended)
    for part in arrived:
        own = own + part
    for mask in bits_of(n_dp):
        if mask >= group:
            own = own + swap(own, {"dp": mask})
    own = own / n_dp

    sketches = [own] + [swap(own, {"dp": s}) for s in range(1, group)]
    right = right_term(who, own, blended, 0, 1.0 / n_dp, group / n_dp)
    for s in range(group - 1, 0, -1):
        right = right_term(who, sketches[s], blended, s, 1.0 / n_dp, group / n_dp, right)

    core = [("rows", 1)]
    plane = [("rows", m) for m in bits_of(n_rows)[1:]] + [("dp", 1)]
    right = scatter_sum(right, core)
    right = scatter_sum(right, plane)
    for mask in bits_of(n_dp)[1:]:
        right = right + swap(right, {"dp": mask})
    right = gather(right, plane)
    right = gather(right, core)

    inverse = factor(right[:, kv:])
    scale = math.sqrt(local_rows * n_rows * kv / rank)
    new_momentum, new_basis, update = finish(
        who, right[:, :kv], inverse, blended, sketches, n_dp, n_rows, scale
    )
    return (new_momentum[None], new_basis, update)


def solution(mesh):
    in_specs = (P("dp", "rows"), P("dp", None), P("dp", "rows", None), P())
    out_specs = (P("dp", "rows", None), P("rows", None), P(("rows", "dp"), None))
    return jax.shard_map(body, mesh=mesh, in_specs=in_specs, out_specs=out_specs, check_vma=False)
```

```python
import functools
import math

import jax
import jax.numpy as jnp
from jax import lax
from jax.experimental import pallas as pl
from jax.experimental.pallas import tpu as pltpu
from jax.sharding import PartitionSpec as P

VMEM_LIMIT = 48 * 1024 * 1024
EXACT = lax.Precision.HIGHEST


def split(value):
    high = value.astype(jnp.bfloat16)
    return high, (value - high.astype(jnp.float32)).astype(jnp.bfloat16)


def dot(left, right, left_dim, right_dim, precision=None):
    return lax.dot_general(
        left,
        right,
        (((left_dim,), (right_dim,)), ((), ())),
        precision=precision,
        preferred_element_type=jnp.float32,
    )


def params(**more):
    return pltpu.CompilerParams(vmem_limit_bytes=VMEM_LIMIT, **more)


def swap(value, masks):
    axes = tuple(a for a in ("dp", "rows") if a in masks)
    sizes = [lax.axis_size(a) for a in axes]
    pairs = []
    for index in range(math.prod(sizes)):
        rest, there = index, 0
        coords = []
        for size in sizes[::-1]:
            coords.append(rest % size)
            rest //= size
        for axis, size, coord in zip(axes, sizes, coords[::-1]):
            there = there * size + (coord ^ masks[axis])
        pairs.append((index, there))
    return lax.ppermute(value, axes, pairs)


def bits_of(count):
    return [1 << b for b in range(count.bit_length() - 1)]


def bit_set(axis, mask):
    return jnp.where((lax.axis_index(axis) & mask) != 0, 1, 0).astype(jnp.int32)


def masks_of(chosen):
    masks = {}
    for axis, mask in chosen:
        masks[axis] = masks.get(axis, 0) | mask
    return masks


def scatter_sum(value, directions):
    count = 1 << len(directions)
    block = value.shape[0] // count
    mine = sum(bit_set(a, m) << b for b, (a, m) in enumerate(directions))
    parts = []
    for s in range(count - 1, 0, -1):
        give = lax.dynamic_slice_in_dim(value, (mine ^ s) * block, block, 0)
        parts.append(swap(give, masks_of([d for b, d in enumerate(directions) if s >> b & 1])))
    total = lax.dynamic_slice_in_dim(value, mine * block, block, 0)
    for part in parts:
        total = total + part
    return total


def gather(value, directions):
    count = 1 << len(directions)
    block = value.shape[0]
    mine = sum(bit_set(a, m) << b for b, (a, m) in enumerate(directions))
    parts = [value] + [
        swap(value, masks_of([d for b, d in enumerate(directions) if s >> b & 1])) for s in range(1, count)
    ]
    out = jnp.zeros((count * block,) + value.shape[1:], value.dtype)
    for s, part in enumerate(parts):
        out = lax.dynamic_update_slice_in_dim(out, part, (mine ^ s) * block, 0)
    return out


VMEM = pl.BlockSpec(memory_space=pltpu.VMEM)
ANY = pl.BlockSpec(memory_space=pl.ANY)
SMEM = pl.BlockSpec(memory_space=pltpu.SMEM)
PARTS = 2


def blend_kernel(first, count, who, acts, grads, momentum, basis, *refs):
    load = count > 1
    blended = refs[0]
    held = refs[1] if load else grads
    sketches = refs[1 + load : 1 + load + PARTS * count]
    acts_held, acts_sem, grads_sem, momentum_sem = refs[1 + load + PARTS * count :]
    tokens, block = acts_held.shape[1:]
    rank = basis.shape[1]
    chunk = tokens // 2
    part = block // PARTS
    starts = [pl.multiple_of((who[0] ^ (first - i)) * block, block) for i in range(count)]

    def acts_copy(i, c):
        here = pl.ds(c * chunk, chunk)
        return pltpu.make_async_copy(
            acts.at[here, pl.ds(starts[i], block)], acts_held.at[i, here], acts_sem.at[i, c]
        )

    def grads_copy(c):
        here = pl.ds(c * chunk, chunk)
        return pltpu.make_async_copy(grads.at[here], held.at[here], grads_sem.at[c])

    def momentum_copy(i):
        return pltpu.make_async_copy(
            momentum.at[pl.ds(starts[i], block)], blended.at[pl.ds(i * block, block)], momentum_sem.at[i]
        )

    for c in range(2):
        acts_copy(0, c).start()
        if load:
            grads_copy(c).start()
    basis_high, basis_low = split(basis[...])
    both = jnp.concatenate([basis_high, basis_low], 1)

    def sketch(index, value):
        high, low = split(value)
        wide = dot(high, both, 1, 0)
        sketches[index][...] = wide[:, :rank] + wide[:, rank:] + dot(low, basis_high, 1, 0)

    pending = None
    for i in range(count):
        columns = [slice(p * part, (p + 1) * part) for p in range(PARTS)]
        if i == 0:
            sums = []
            for c in range(2):
                acts_copy(0, c).wait()
                if load:
                    grads_copy(c).wait()
                if c == 0:
                    momentum_copy(0).start()
                elif count > 1:
                    for d in range(2):
                        acts_copy(1, d).start()
                    momentum_copy(1).start()
                here = slice(c * chunk, (c + 1) * chunk)
                terms = [dot(acts_held[0, here, cols], held[here, :], 0, 0) for cols in columns]
                sums = terms if c == 0 else [a + b for a, b in zip(sums, terms)]
        else:
            for c in range(2):
                acts_copy(i, c).wait()
            if i + 1 < count:
                for d in range(2):
                    acts_copy(i + 1, d).start()
                momentum_copy(i + 1).start()
        momentum_copy(i).wait()
        for p, cols in enumerate(columns):
            rows = slice(i * block + p * part, i * block + (p + 1) * part)
            gradient = sums[p] if i == 0 else dot(acts_held[i, :, cols], held[...], 0, 0)
            value = blended[rows, :] + gradient
            blended[rows, :] = value
            if pending is not None:
                sketch(*pending)
            pending = (i * PARTS + p, value)
    sketch(*pending)


def blend(who, acts, grads, momentum, basis, group, first, count):
    tokens, rows = acts.shape
    kv, rank = basis.shape
    block = rows // group
    load = count > 1
    outs = [pltpu.VMEM((count * block, kv), jnp.float32)]
    if load:
        outs.append(pltpu.VMEM((tokens, kv), jnp.bfloat16))
    outs += [jax.ShapeDtypeStruct((block // PARTS, rank), jnp.float32)] * (PARTS * count)
    out = pl.pallas_call(
        functools.partial(blend_kernel, first, count),
        in_specs=[SMEM, ANY, ANY if load else VMEM, ANY, VMEM],
        out_specs=[VMEM] * len(outs),
        out_shape=outs,
        scratch_shapes=[
            pltpu.VMEM((count, tokens, block), jnp.bfloat16),
            pltpu.SemaphoreType.DMA((count, 2)),
            pltpu.SemaphoreType.DMA((2,)),
            pltpu.SemaphoreType.DMA((count,)),
        ],
        compiler_params=params(),
        cost_estimate=pl.CostEstimate(
            flops=2 * count * block * tokens * kv, bytes_accessed=4 * count * block * kv * 3, transcendentals=0
        ),
        name="blend",
    )(who, acts, grads, momentum, basis)
    return out[0], out[1 : 1 + load], out[1 + load :]


def right_product(sketch, blended):
    turned = sketch.T
    rank = turned.shape[0]
    high, low = split(turned)
    stacked = jnp.concatenate([high, low], 0)
    blended_high, blended_low = split(blended)
    wide = dot(stacked, blended_high, 1, 0)
    gram = dot(stacked, stacked, 1, 1)
    gram = gram[:rank, :rank] + gram[rank:, rank:] + (gram[:rank, rank:] + gram[rank:, :rank])
    return wide[:rank] + wide[rank:] + dot(high, blended_low, 1, 0), gram


def right_kernel(pieces, last, scale, *refs):
    who, blended = refs[:2]
    refs = refs[2:]
    sketches, refs = refs[: len(pieces)], refs[len(pieces) :]
    right, gram = None, None
    for (start, rows), sketch in zip(pieces, sketches):
        right_term, gram_term = right_product(sketch[...], blended[start : start + rows, :])
        right = right_term if right is None else right + right_term
        gram = gram_term if gram is None else gram + gram_term
    right = scale * right
    if not last:
        refs[0][...] = right
        refs[1][...] = gram
        return
    befores, refs = refs[:-4], refs[-4:]
    keep, give, gram_out, total = refs
    for before in befores[::2]:
        right = right + before[...]
    for before in befores[1::2]:
        gram = gram + before[...]
    gram_out[...] = gram
    total[...] = right
    half = keep.shape[0]
    core = who[2] & 1
    keep[...] = total[pl.ds(pl.multiple_of(core * half, half), half), :]
    give[...] = total[pl.ds(pl.multiple_of((1 - core) * half, half), half), :]


def right_terms(who, blended, pieces, sketches, scale, befores=None):
    rank = sketches[0].shape[1]
    kv = blended.shape[1]
    last = befores is not None
    gram = jax.ShapeDtypeStruct((rank, rank), jnp.float32)
    if last:
        outs = [jax.ShapeDtypeStruct((rank // 2, kv), jnp.float32)] * 2 + [gram]
    else:
        outs = [pltpu.VMEM((rank, kv), jnp.float32), pltpu.VMEM((rank, rank), jnp.float32)]
    operands = [who, blended, *sketches, *(befores or [])]
    return pl.pallas_call(
        functools.partial(right_kernel, pieces, last, scale),
        in_specs=[SMEM] + [VMEM] * (len(operands) - 1),
        out_specs=[VMEM] * len(outs),
        out_shape=outs,
        scratch_shapes=[pltpu.VMEM((rank, kv), jnp.float32)] if last else [],
        compiler_params=params(),
        cost_estimate=pl.CostEstimate(
            flops=6 * sum(r for _, r in pieces) * rank * kv,
            bytes_accessed=4 * rank * kv,
            transcendentals=0,
        ),
        name="right_terms",
    )(*operands)


PANEL = 16


def factor_kernel(panels, fresh, *refs):
    rank = refs[0].shape[0]
    if fresh:
        gram_a, gram_b, out = refs
        rows_id = lax.broadcasted_iota(jnp.int32, (rank, rank), 0)
        cols_id = lax.broadcasted_iota(jnp.int32, (rank, rank), 1)
        out[:, :rank] = gram_a[...] + gram_b[...]
        out[:, rank:] = jnp.where(rows_id == cols_id, 1.0, 0.0)
    else:
        out = refs[1]
        out[...] = refs[0][...]
    index = lax.broadcasted_iota(jnp.int32, (PANEL, rank), 0)
    for start in panels:
        here = slice(start, start + PANEL)
        left = out[here, :rank]
        right = out[here, rank:]
        columns = [
            jnp.broadcast_to(left[:, start + c : start + c + 1], (PANEL, rank)) for c in range(PANEL)
        ]
        pivots = jnp.ones((PANEL, rank), jnp.float32)
        for j in range(PANEL):
            pivot = columns[j][j : j + 1, :]
            pivots = jnp.where(index == j, pivot, pivots)
            factor = jnp.where(index > j, columns[j] * (1.0 / pivot), 0.0)
            for c in range(j + 1, PANEL):
                columns[c] = columns[c] - factor * columns[c][j : j + 1, :]
            left = left - factor * left[j : j + 1, :]
            right = right - factor * right[j : j + 1, :]
        weight = 1.0 / jnp.sqrt(pivots)
        left = left * weight
        right = right * weight
        out[here, :rank] = left
        out[here, rank:] = right
        if start + PANEL < rank:
            rows = jnp.concatenate([left, right], 1)
            high, rest = split(rows)
            middle = rest
            low = (rows - high.astype(jnp.float32) - middle.astype(jnp.float32)).astype(jnp.bfloat16)
            one = jnp.concatenate([high, high, middle, middle, high, low], 0)[:, :rank]
            two = jnp.concatenate([high, middle, high, middle, low, high], 0)
            update = dot(one, two, 0, 0)
            below = slice(start + PANEL, rank)
            out[below, :] = out[below, :] - update[start + PANEL :, :]


def factor(panels, *inputs):
    rank = inputs[0].shape[0]
    return pl.pallas_call(
        functools.partial(factor_kernel, panels, len(inputs) == 2),
        in_specs=[VMEM] * len(inputs),
        out_specs=VMEM,
        out_shape=pltpu.VMEM((rank, 2 * rank), jnp.float32),
        compiler_params=params(),
        cost_estimate=pl.CostEstimate(flops=2 * 10**9, bytes_accessed=10**6, transcendentals=0),
        name="factor",
    )(*inputs)


def ortho_kernel(group, who, state, *refs):
    sketches, refs = refs[: PARTS * group], refs[PARTS * group :]
    ortho, own_ortho, total = refs
    rank = state.shape[0]
    part = sketches[0].shape[0]
    inverse = state[:, rank:]
    for s in range(group):
        for p in range(PARTS):
            value = sketches[s * PARTS + p][...]
            high, low = split(value)
            first, second = split(inverse)
            wide = dot(high, jnp.concatenate([first, second], 0), 1, 1)
            value = wide[:, :rank] + wide[:, rank:] + dot(low, first, 1, 1)
            rows = slice((s * PARTS + p) * part, (s * PARTS + p + 1) * part)
            ortho[rows, :] = jnp.concatenate(split(value), 1)
            start = ((who[0] ^ s) * PARTS + p) * part
            total[pl.ds(pl.multiple_of(start, part), part), :] = value
    own = own_ortho.shape[0]
    own_ortho[...] = total[pl.ds(pl.multiple_of(who[1] * own, own), own), :]


def orthonormal(who, state, sketches, group, n_dp):
    rank = state.shape[0]
    rows = sketches[0].shape[0] * len(sketches)
    return pl.pallas_call(
        functools.partial(ortho_kernel, group),
        in_specs=[SMEM] + [VMEM] * (1 + len(sketches)),
        out_specs=[VMEM] * 2,
        out_shape=[
            pltpu.VMEM((rows, 2 * rank), jnp.bfloat16),
            pltpu.VMEM((rows // n_dp, rank), jnp.float32),
        ],
        scratch_shapes=[pltpu.VMEM((rows, rank), jnp.float32)],
        compiler_params=params(),
        cost_estimate=pl.CostEstimate(flops=10**9, bytes_accessed=10**6, transcendentals=0),
        name="ortho",
    )(who, state, *sketches)


def finish_kernel(group, scale, who, right, state, ortho, own_ortho, own_blended, other_blended, *refs):
    new_momentum, new_basis, update, coeff, coeff_high, coeff_low = refs
    step = pl.program_id(0)
    block = own_blended.shape[0]
    rank, kv = right.shape

    @pl.when(step == 0)
    def _():
        value = dot(state[:, rank:], right[...], 1, 0, EXACT)
        coeff[...] = value
        high, low = split(0.2 * value)
        coeff_high[:rank, :] = high
        coeff_high[rank:, :] = high
        coeff_low[...] = low

    def feedback(s):
        rows = ortho[s * block : (s + 1) * block, :]
        return dot(rows, coeff_high[...], 1, 0) + dot(rows[:, :rank], coeff_low[...], 1, 0)

    for s in range(group):

        @pl.when(step == s)
        def _(s=s):
            if s == 0:
                before = own_blended[...]
            else:
                at = (group - 1 - s) * block
                before = other_blended[at : at + block, :]
            new_momentum[...] = before - feedback(s)

    @pl.when(step == group - 1)
    def _():
        value = coeff[...]
        norm = jnp.sqrt(jnp.sum(value * value, axis=1, keepdims=True) + 1e-06)
        normed = value / norm
        count = new_basis.shape[0]
        for j in range(kv // count):

            @pl.when(who[2] == j)
            def _(j=j):
                new_basis[...] = normed[:, j * count : (j + 1) * count].T

        rows_high, rows_low = split(own_ortho[...])
        high, low = split(normed)
        product = dot(jnp.concatenate([rows_high, rows_low], 1), jnp.concatenate([high, high], 0), 1, 0)
        update[...] = (scale * (product + dot(rows_high, low, 1, 0))).astype(update.dtype)


def finish(who, right, state, ortho, own_ortho, own_blended, other_blended, group, n_rows, scale):
    rank, kv = right.shape
    block = own_blended.shape[0]
    rows = block * group
    const = lambda i, who: (0, 0)
    return pl.pallas_call(
        functools.partial(finish_kernel, group, scale),
        grid_spec=pltpu.PrefetchScalarGridSpec(
            num_scalar_prefetch=1,
            grid=(group,),
            in_specs=[VMEM] * 6,
            out_specs=[
                pl.BlockSpec((block, kv), lambda i, who: (who[0] ^ i, 0)),
                pl.BlockSpec((kv // n_rows, rank), const),
                pl.BlockSpec(own_ortho.shape[:1] + (kv,), const),
            ],
            scratch_shapes=[
                pltpu.VMEM((rank, kv), jnp.float32),
                pltpu.VMEM((2 * rank, kv), jnp.bfloat16),
                pltpu.VMEM((rank, kv), jnp.bfloat16),
            ],
        ),
        out_shape=[
            jax.ShapeDtypeStruct((rows, kv), jnp.float32),
            jax.ShapeDtypeStruct((kv // n_rows, rank), jnp.float32),
            jax.ShapeDtypeStruct(own_ortho.shape[:1] + (kv,), jnp.bfloat16),
        ],
        compiler_params=params(),
        name="finish",
    )(who, right, state, ortho, own_ortho, own_blended, other_blended)


def body(activations, key_grads, momentum, basis):
    n_dp = lax.axis_size("dp")
    n_rows = lax.axis_size("rows")
    dp = lax.axis_index("dp")
    group = min(4, n_dp)
    low = dp & (group - 1)
    who = jnp.stack([low, dp, lax.axis_index("rows")]).astype(jnp.int32)
    kv, rank = basis.shape
    local_rows = activations.shape[1]
    block = local_rows // group
    part = block // PARTS
    far = [mask for mask in bits_of(n_dp) if mask >= group]

    other_blended, held, others = blend(who, activations, key_grads, momentum[0], basis, group, group - 1, group - 1)
    arrived = []
    for p in range(PARTS):
        arrived.append([swap(others[i * PARTS + p], {"dp": group - 1 - i}) for i in range(group - 1)])
    own_blended, _, own = blend(who, activations, held[0], momentum[0], basis, group, 0, 1)
    own = list(own)
    sketches = [[None] * PARTS for _ in range(group)]
    for p in range(PARTS):
        for piece in arrived[p]:
            own[p] = own[p] + piece
        for mask in far:
            own[p] = own[p] + swap(own[p], {"dp": mask})
        own[p] = own[p] * (1.0 / n_dp)
        sketches[0][p] = own[p]
        for s in range(group - 1, 0, -1):
            sketches[s][p] = swap(own[p], {"dp": s})

    scale = 1.0 / n_dp
    befores = list(right_terms(who, own_blended, [(p * part, part) for p in range(PARTS)], own, scale))
    for p in range(PARTS):
        pieces = [((group - 1 - s) * block + p * part, part) for s in range(1, group)]
        given = [sketches[s][p] for s in range(1, group)]
        if p + 1 < PARTS:
            befores += right_terms(who, other_blended, pieces, given, scale)
        else:
            keep, give, gram = right_terms(who, other_blended, pieces, given, scale, befores)

    right = keep + swap(give, {"rows": 1})
    gram = gram + swap(gram, {"rows": 1})
    plane = [("rows", m) for m in bits_of(n_rows)[1:]] + [("dp", 1)]
    row_masks = bits_of(n_rows)[1:]
    for mask in row_masks[:-1]:
        gram = gram + swap(gram, {"rows": mask})
    gram_other = swap(gram, {"rows": row_masks[-1]})
    right = scatter_sum(right, plane)
    panels = list(range(0, rank, PANEL))
    middle = len(panels) // 2
    right, gram, gram_other = lax.optimization_barrier((right, gram, gram_other))
    state = None
    for step, mask in enumerate(bits_of(n_dp)[1:]):
        other = swap(right, {"dp": mask})
        if step == 0:
            state = factor(panels[:middle], gram, gram_other)
        elif step == 1:
            state = factor(panels[middle:], state)
        right, state = lax.optimization_barrier((right + other, state))
    flat = [sketches[s][p] for s in range(group) for p in range(PARTS)]
    right = gather(right, plane)
    ortho, own_ortho = orthonormal(who, state, flat, group, n_dp)
    right = gather(right, [("rows", 1)])

    new_momentum, new_basis, update = finish(
        who, right, state, ortho, own_ortho, own_blended, other_blended, group, n_rows,
        math.sqrt(local_rows * n_rows * kv / rank),
    )
    return (new_momentum[None], new_basis, update)


def solution(mesh):
    in_specs = (P("dp", "rows"), P("dp", None), P("dp", "rows", None), P())
    out_specs = (P("dp", "rows", None), P("rows", None), P(("rows", "dp"), None))
    return jax.shard_map(body, mesh=mesh, in_specs=in_specs, out_specs=out_specs, check_vma=False)
```

```python
import functools
import math

import jax
import jax.numpy as jnp
from jax import lax
from jax.experimental import pallas as pl
from jax.experimental.pallas import tpu as pltpu
from jax.sharding import PartitionSpec as P

MIB = 1024 * 1024
FIRST_MIB = 44
BLEND_MIB = 40
EXACT = lax.Precision.HIGHEST


def split(value):
    high = value.astype(jnp.bfloat16)
    return high, (value - high.astype(jnp.float32)).astype(jnp.bfloat16)


def dot(left, right, left_dim, right_dim, precision=None):
    return lax.dot_general(
        left,
        right,
        (((left_dim,), (right_dim,)), ((), ())),
        precision=precision,
        preferred_element_type=jnp.float32,
    )


def params(mib):
    return pltpu.CompilerParams(vmem_limit_bytes=mib * MIB)


def swap(value, masks):
    axes = tuple(a for a in ("dp", "rows") if a in masks)
    sizes = [lax.axis_size(a) for a in axes]
    pairs = []
    for index in range(math.prod(sizes)):
        rest, there = index, 0
        coords = []
        for size in sizes[::-1]:
            coords.append(rest % size)
            rest //= size
        for axis, size, coord in zip(axes, sizes, coords[::-1]):
            there = there * size + (coord ^ masks[axis])
        pairs.append((index, there))
    return lax.ppermute(value, axes, pairs)


def bits_of(count):
    return [1 << b for b in range(count.bit_length() - 1)]


def bit_set(axis, mask):
    return jnp.where((lax.axis_index(axis) & mask) != 0, 1, 0).astype(jnp.int32)


def masks_of(chosen):
    masks = {}
    for axis, mask in chosen:
        masks[axis] = masks.get(axis, 0) | mask
    return masks


def gather(value, directions, beside):
    count = 1 << len(directions)
    block = value.shape[0]
    mine = sum(bit_set(a, m) << b for b, (a, m) in enumerate(directions))
    parts = [value] + [
        swap(value, masks_of([d for b, d in enumerate(directions) if s >> b & 1])) for s in range(1, count)
    ]
    *parts, beside = lax.optimization_barrier((*parts, beside))
    out = jnp.zeros((count * block,) + value.shape[1:], value.dtype)
    for s, part in enumerate(parts):
        out = lax.dynamic_update_slice_in_dim(out, part, (mine ^ s) * block, 0)
    return out, beside


VMEM = pl.BlockSpec(memory_space=pltpu.VMEM)
ANY = pl.BlockSpec(memory_space=pl.ANY)
SMEM = pl.BlockSpec(memory_space=pltpu.SMEM)
PARTS = 2


def sketch_of(value, both, rank):
    high, low = split(value)
    wide = dot(high, both, 1, 0)
    return wide[:, :rank] + wide[:, rank:] + dot(low, both[:, :rank], 1, 0)


CHUNKS = 4


def first_blend_kernel(group, offsets, later, acts, grads, momentum, basis, *refs):
    count, extra = len(offsets), len(later)
    blended, held, acts_later = refs[:3]
    momentum_later = refs[3 : 3 + extra]
    sketches = refs[3 + extra : 3 + extra + PARTS * count]
    refs = refs[3 + extra + PARTS * count :]
    acts_held, values, both, acts_sem, grads_sem, momentum_sem, later_sem, out_sem = refs
    low = lax.axis_index("dp") & (group - 1)
    tokens, block = acts_held.shape[1:]
    rank = basis.shape[1]
    chunk = tokens // CHUNKS
    part = block // PARTS

    def start_of(offset):
        return pl.multiple_of((low ^ offset) * block, block)

    def acts_copy(i, c):
        here = pl.ds(c * chunk, chunk)
        return pltpu.make_async_copy(
            acts.at[here, pl.ds(start_of(offsets[i]), block)], acts_held.at[i, here], acts_sem.at[i, c]
        )

    def grads_copy(c):
        here = pl.ds(c * chunk, chunk)
        return pltpu.make_async_copy(grads.at[here], held.at[here], grads_sem.at[c])

    def momentum_copy(i):
        return pltpu.make_async_copy(
            momentum.at[pl.ds(start_of(offsets[i]), block)],
            values.at[pl.ds(i * block, block)],
            momentum_sem.at[i],
        )

    def out_copy(index):
        here = pl.ds(index * part, part)
        return pltpu.make_async_copy(values.at[here], blended.at[here], out_sem.at[index])

    def later_copies(i):
        here = pl.ds(start_of(later[i]), block)
        return [
            pltpu.make_async_copy(acts.at[:, here], acts_later.at[i], later_sem.at[i, 0]),
            pltpu.make_async_copy(momentum.at[here], momentum_later[i], later_sem.at[i, 1]),
        ]

    for c in range(CHUNKS):
        acts_copy(0, c).start()
        grads_copy(c).start()
    basis_high, basis_low = split(basis[...])
    both[:, :rank] = basis_high
    both[:, rank:] = basis_low
    columns = [slice(p * part, (p + 1) * part) for p in range(PARTS)]
    pending = None
    for i in range(count):
        if i == 0:
            sums = None
            for c in range(CHUNKS):
                acts_copy(0, c).wait()
                grads_copy(c).wait()
                if c == CHUNKS // 2:
                    momentum_copy(0).start()
                here = slice(c * chunk, (c + 1) * chunk)
                terms = [dot(acts_held[0, here, cols], held[here, :], 0, 0) for cols in columns]
                sums = terms if c == 0 else [a + b for a, b in zip(sums, terms)]
        else:
            for c in range(CHUNKS):
                acts_copy(i, c).wait()
        if i + 1 < count:
            for c in range(CHUNKS):
                acts_copy(i + 1, c).start()
            momentum_copy(i + 1).start()
        else:
            for n in range(extra):
                for copy in later_copies(n):
                    copy.start()
        momentum_copy(i).wait()
        for p, cols in enumerate(columns):
            rows = slice(i * block + p * part, i * block + (p + 1) * part)
            gradient = sums[p] if i == 0 else dot(acts_held[i, :, cols], held[...], 0, 0)
            value = values[rows, :] + gradient
            values[rows, :] = value
            if pending is not None:
                out_copy(pending[0]).start()
                sketches[pending[0]][...] = sketch_of(pending[1], both[...], rank)
            pending = (i * PARTS + p, value)
    out_copy(pending[0]).start()
    sketches[pending[0]][...] = sketch_of(pending[1], both[...], rank)
    for index in range(count * PARTS):
        out_copy(index).wait()
    for n in range(extra):
        for copy in later_copies(n):
            copy.wait()


def first_blend(acts, grads, momentum, basis, group, offsets, later):
    tokens, rows = acts.shape
    kv, rank = basis.shape
    block = rows // group
    count, extra = len(offsets), len(later)
    outs = [
        jax.ShapeDtypeStruct((rows, kv), jnp.float32),
        pltpu.VMEM((tokens, kv), jnp.bfloat16),
        pltpu.VMEM((extra, tokens, block), jnp.bfloat16),
    ]
    outs += [pltpu.VMEM((block, kv), jnp.float32)] * extra
    outs += [pltpu.VMEM((block // PARTS, rank), jnp.float32)] * (PARTS * count)
    out = pl.pallas_call(
        functools.partial(first_blend_kernel, group, offsets, later),
        in_specs=[ANY, ANY, ANY, VMEM],
        out_specs=[ANY] + [VMEM] * (len(outs) - 1),
        out_shape=outs,
        scratch_shapes=[
            pltpu.VMEM((count, tokens, block), jnp.bfloat16),
            pltpu.VMEM((count * block, kv), jnp.float32),
            pltpu.VMEM((kv, 2 * rank), jnp.bfloat16),
            pltpu.SemaphoreType.DMA((count, CHUNKS)),
            pltpu.SemaphoreType.DMA((CHUNKS,)),
            pltpu.SemaphoreType.DMA((count,)),
            pltpu.SemaphoreType.DMA((extra, 2)),
            pltpu.SemaphoreType.DMA((count * PARTS,)),
        ],
        compiler_params=params(FIRST_MIB),
        name="first_blend",
    )(acts, grads, momentum, basis)
    return out[0], out[1], out[2], out[3 : 3 + extra], out[3 + extra :]


def blend_kernel(index, first, acts, grads, basis, momentum, _, blended, *refs):
    sketches, (values, out_sem) = refs[:PARTS], refs[PARTS:]
    block = acts.shape[2]
    rank = basis.shape[1]
    part = block // PARTS
    both = jnp.concatenate(split(basis[...]), 1)

    def out_copy(p):
        return pltpu.make_async_copy(
            values.at[pl.ds(p * part, part)], blended.at[pl.ds(first + p * part, part)], out_sem.at[p]
        )

    pending = None
    for p in range(PARTS):
        rows = slice(p * part, (p + 1) * part)
        value = momentum[rows, :] + dot(acts[index, :, rows], grads[...], 0, 0)
        values[rows, :] = value
        if pending is not None:
            out_copy(p - 1).start()
            sketches[p - 1][...] = sketch_of(pending, both, rank)
        pending = value
    out_copy(PARTS - 1).start()
    sketches[PARTS - 1][...] = sketch_of(pending, both, rank)
    for p in range(PARTS):
        out_copy(p).wait()


def blend(acts, grads, basis, momentum, blended, index, first):
    block = acts.shape[2]
    kv, rank = basis.shape
    outs = [jax.ShapeDtypeStruct(blended.shape, jnp.float32)]
    outs += [pltpu.VMEM((block // PARTS, rank), jnp.float32)] * PARTS
    out = pl.pallas_call(
        functools.partial(blend_kernel, index, first),
        in_specs=[VMEM] * 4 + [ANY],
        out_specs=[ANY] + [VMEM] * PARTS,
        out_shape=outs,
        scratch_shapes=[pltpu.VMEM((block, kv), jnp.float32), pltpu.SemaphoreType.DMA((PARTS,))],
        input_output_aliases={4: 0},
        compiler_params=params(BLEND_MIB),
        name="blend",
    )(acts, grads, basis, momentum, blended)
    return out[0], out[1:]


def right_product(sketch, blended):
    turned = sketch.T
    rank = turned.shape[0]
    high, low = split(turned)
    stacked = jnp.concatenate([high, low], 0)
    blended_high, blended_low = split(blended)
    wide = dot(stacked, blended_high, 1, 0)
    gram = dot(stacked, stacked, 1, 1)
    gram = gram[:rank, :rank] + gram[rank:, rank:] + (gram[:rank, rank:] + gram[rank:, :rank])
    return wide[:rank] + wide[rank:] + dot(high, blended_low, 1, 0), gram


def right_kernel(pieces, first, last, scale, *refs):
    who, blended = refs[:2]
    refs = refs[2:]
    sketches, refs = refs[: len(pieces)], refs[len(pieces) :]
    if first:
        held, sem = refs[-2:]
        start, rows = pieces[0][0], sum(r for _, r in pieces)
        copies = []
        for at, size in ((start, rows), (0, start), (start + rows, blended.shape[0] - start - rows)):
            if size:
                here = pl.ds(at, size)
                copies.append(pltpu.make_async_copy(blended.at[here], held.at[here], sem.at[len(copies)]))
                copies[-1].start()
        copies[0].wait()
        blended = held
    right, gram = None, None
    for (start, rows), sketch in zip(pieces, sketches):
        right_term, gram_term = right_product(sketch[...], blended[start : start + rows, :])
        right = right_term if right is None else right + right_term
        gram = gram_term if gram is None else gram + gram_term
    right = scale * right
    if not last:
        refs[0][...] = right
        refs[1][...] = gram
        if first:
            for copy in copies[1:]:
                copy.wait()
        return
    befores, refs = refs[:-4], refs[-4:]
    keep, give, gram_out, total = refs
    for before in befores[::2]:
        right = right + before[...]
    for before in befores[1::2]:
        gram = gram + before[...]
    gram_out[...] = gram
    total[...] = right
    half = keep.shape[0]
    core = who[2] & 1
    keep[...] = total[pl.ds(pl.multiple_of(core * half, half), half), :]
    give[...] = total[pl.ds(pl.multiple_of((1 - core) * half, half), half), :]


def right_terms(who, blended, pieces, sketches, scale, befores=None, first=False):
    rank = sketches[0].shape[1]
    kv = blended.shape[1]
    last = befores is not None
    gram = pltpu.VMEM((rank, rank), jnp.float32)
    if last:
        outs = [pltpu.VMEM((rank // 2, kv), jnp.float32)] * 2 + [gram]
    else:
        outs = [pltpu.VMEM((rank, kv), jnp.float32), pltpu.VMEM((rank, rank), jnp.float32)]
    scratch = [pltpu.VMEM((rank, kv), jnp.float32)] if last else []
    if first:
        outs.append(pltpu.VMEM(blended.shape, jnp.float32))
        scratch = [pltpu.SemaphoreType.DMA((3,))]
    operands = [who, blended, *sketches, *(befores or [])]
    return pl.pallas_call(
        functools.partial(right_kernel, pieces, first, last, scale),
        in_specs=[SMEM, ANY if first else VMEM] + [VMEM] * (len(operands) - 2),
        out_specs=[VMEM] * len(outs),
        out_shape=outs,
        scratch_shapes=scratch,
        compiler_params=params(FIRST_MIB if first else 16),
        name="right_terms",
    )(*operands)


def cut_kernel(count, who, keep, arrived, *blocks):
    block = blocks[0].shape[0]
    for s, out in enumerate(blocks):
        here = pl.ds(pl.multiple_of((who[3] ^ s) * block, block), block)
        out[...] = keep[here, :] + arrived[here, :]


def cut(who, keep, arrived, count):
    rows, kv = keep.shape
    return pl.pallas_call(
        functools.partial(cut_kernel, count),
        in_specs=[SMEM, VMEM, VMEM],
        out_specs=[VMEM] * count,
        out_shape=[pltpu.VMEM((rows // count, kv), jnp.float32)] * count,
        compiler_params=params(16),
        name="cut",
    )(who, keep, arrived)


PANEL = 16


def factor_kernel(panels, fresh, *refs):
    rank = refs[0].shape[0]
    if fresh:
        gram_a, gram_b, out = refs
        rows_id = lax.broadcasted_iota(jnp.int32, (rank, rank), 0)
        cols_id = lax.broadcasted_iota(jnp.int32, (rank, rank), 1)
        out[:, :rank] = gram_a[...] + gram_b[...]
        out[:, rank:] = jnp.where(rows_id == cols_id, 1.0, 0.0)
    else:
        out = refs[1]
        out[...] = refs[0][...]
    index = lax.broadcasted_iota(jnp.int32, (PANEL, rank), 0)
    for start in panels:
        here = slice(start, start + PANEL)
        left = out[here, :rank]
        right = out[here, rank:]
        columns = [
            jnp.broadcast_to(left[:, start + c : start + c + 1], (PANEL, rank)) for c in range(PANEL)
        ]
        pivots = jnp.ones((PANEL, rank), jnp.float32)
        for j in range(PANEL):
            pivot = columns[j][j : j + 1, :]
            pivots = jnp.where(index == j, pivot, pivots)
            factor = jnp.where(index > j, columns[j] * (1.0 / pivot), 0.0)
            for c in range(j + 1, PANEL):
                columns[c] = columns[c] - factor * columns[c][j : j + 1, :]
            left = left - factor * left[j : j + 1, :]
            right = right - factor * right[j : j + 1, :]
        weight = 1.0 / jnp.sqrt(pivots)
        left = left * weight
        right = right * weight
        out[here, :rank] = left
        out[here, rank:] = right
        if start + PANEL < rank:
            rows = jnp.concatenate([left, right], 1)
            high, rest = split(rows)
            middle = rest
            low = (rows - high.astype(jnp.float32) - middle.astype(jnp.float32)).astype(jnp.bfloat16)
            one = jnp.concatenate([high, high, middle, middle, high, low], 0)[:, :rank]
            two = jnp.concatenate([high, middle, high, middle, low, high], 0)
            update = dot(one, two, 0, 0)
            below = slice(start + PANEL, rank)
            out[below, :] = out[below, :] - update[start + PANEL :, :]


def factor(panels, *inputs):
    rank = inputs[0].shape[0]
    return pl.pallas_call(
        functools.partial(factor_kernel, panels, len(inputs) == 2),
        in_specs=[VMEM] * len(inputs),
        out_specs=VMEM,
        out_shape=pltpu.VMEM((rank, 2 * rank), jnp.float32),
        compiler_params=params(16),
        name="factor",
    )(*inputs)


def ortho_kernel(group, who, state, *refs):
    sketches, refs = refs[: PARTS * group], refs[PARTS * group :]
    blended, ortho, own_ortho, held, total, sem = refs
    copy = pltpu.make_async_copy(blended, held, sem)
    copy.start()
    rank = state.shape[0]
    part = sketches[0].shape[0]
    inverse = state[:, rank:]
    for s in range(group):
        for p in range(PARTS):
            value = sketches[s * PARTS + p][...]
            high, low = split(value)
            first, second = split(inverse)
            wide = dot(high, jnp.concatenate([first, second], 0), 1, 1)
            value = wide[:, :rank] + wide[:, rank:] + dot(low, first, 1, 1)
            rows = slice((s * PARTS + p) * part, (s * PARTS + p + 1) * part)
            ortho[rows, :] = jnp.concatenate(split(value), 1)
            start = ((who[0] ^ s) * PARTS + p) * part
            total[pl.ds(pl.multiple_of(start, part), part), :] = value
    own = own_ortho.shape[0]
    own_ortho[...] = total[pl.ds(pl.multiple_of(who[1] * own, own), own), :]
    copy.wait()


def orthonormal(who, state, sketches, blended, group, n_dp):
    rank = state.shape[0]
    rows = sketches[0].shape[0] * len(sketches)
    return pl.pallas_call(
        functools.partial(ortho_kernel, group),
        in_specs=[SMEM] + [VMEM] * (1 + len(sketches)) + [ANY],
        out_specs=[VMEM] * 3,
        out_shape=[
            pltpu.VMEM((rows, 2 * rank), jnp.bfloat16),
            pltpu.VMEM((rows // n_dp, rank), jnp.float32),
            pltpu.VMEM(blended.shape, jnp.float32),
        ],
        scratch_shapes=[pltpu.VMEM((rows, rank), jnp.float32), pltpu.SemaphoreType.DMA],
        compiler_params=params(FIRST_MIB),
        name="ortho",
    )(who, state, *sketches, blended)


def finish_kernel(group, places, scale, who, right_here, right_there, state, ortho, own_ortho, *refs):
    blended, new_momentum, new_basis, update, right, coeff, coeff_high, coeff_low = refs
    step = pl.program_id(0)
    block = new_momentum.shape[0]
    rank, kv = right.shape
    half = rank // 2
    core = who[2] & 1

    @pl.when(step == 0)
    def _():
        right[pl.ds(pl.multiple_of(core * half, half), half), :] = right_here[...]
        right[pl.ds(pl.multiple_of((1 - core) * half, half), half), :] = right_there[...]
        value = dot(state[:, rank:], right[...], 1, 0, EXACT)
        coeff[...] = value
        high, low = split(0.2 * value)
        coeff_high[:rank, :] = high
        coeff_high[rank:, :] = high
        coeff_low[...] = low

    def feedback(s):
        rows = ortho[s * block : (s + 1) * block, :]
        return dot(rows, coeff_high[...], 1, 0) + dot(rows[:, :rank], coeff_low[...], 1, 0)

    for s in range(group):

        @pl.when(step == s)
        def _(s=s):
            new_momentum[...] = blended[places[s] : places[s] + block, :] - feedback(s)

    @pl.when(step == group - 1)
    def _():
        value = coeff[...]
        norm = jnp.sqrt(jnp.sum(value * value, axis=1, keepdims=True) + 1e-06)
        normed = value / norm
        count = new_basis.shape[0]
        for j in range(kv // count):

            @pl.when(who[2] == j)
            def _(j=j):
                new_basis[...] = normed[:, j * count : (j + 1) * count].T

        rows_high, rows_low = split(own_ortho[...])
        high, low = split(normed)
        product = dot(jnp.concatenate([rows_high, rows_low], 1), jnp.concatenate([high, high], 0), 1, 0)
        update[...] = (scale * (product + dot(rows_high, low, 1, 0))).astype(update.dtype)


def finish(who, right_here, right_there, state, ortho, own_ortho, blended, places, n_rows, scale):
    rank, kv = 2 * right_here.shape[0], right_here.shape[1]
    group = len(places)
    rows = ortho.shape[0]
    block = rows // group
    const = lambda i, who: (0, 0)
    return pl.pallas_call(
        functools.partial(finish_kernel, group, places, scale),
        grid_spec=pltpu.PrefetchScalarGridSpec(
            num_scalar_prefetch=1,
            grid=(group,),
            in_specs=[VMEM] * 6,
            out_specs=[
                pl.BlockSpec((block, kv), lambda i, who: (who[0] ^ i, 0)),
                pl.BlockSpec((kv // n_rows, rank), const),
                pl.BlockSpec(own_ortho.shape[:1] + (kv,), const),
            ],
            scratch_shapes=[
                pltpu.VMEM((rank, kv), jnp.float32),
                pltpu.VMEM((rank, kv), jnp.float32),
                pltpu.VMEM((2 * rank, kv), jnp.bfloat16),
                pltpu.VMEM((rank, kv), jnp.bfloat16),
            ],
        ),
        out_shape=[
            jax.ShapeDtypeStruct((rows, kv), jnp.float32),
            jax.ShapeDtypeStruct((kv // n_rows, rank), jnp.float32),
            jax.ShapeDtypeStruct(own_ortho.shape[:1] + (kv,), jnp.bfloat16),
        ],
        compiler_params=params(16),
        name="finish",
    )(who, right_here, right_there, state, ortho, own_ortho, blended)


def body(activations, key_grads, momentum, basis):
    n_dp = lax.axis_size("dp")
    n_rows = lax.axis_size("rows")
    dp = lax.axis_index("dp")
    group = min(4, n_dp)
    low = dp & (group - 1)
    kv, rank = basis.shape
    local_rows = activations.shape[1]
    block = local_rows // group
    part = block // PARTS
    far = [mask for mask in bits_of(n_dp) if mask >= group]
    plane = [("rows", m) for m in bits_of(n_rows)[1:]] + [("dp", 1)]
    mine = sum(bit_set(a, m) << b for b, (a, m) in enumerate(plane))
    who = jnp.stack([low, dp, lax.axis_index("rows"), mine]).astype(jnp.int32)

    offsets, later = tuple(range(group - 1, 1, -1)), (1, 0)
    blended, held, acts_later, momentum_later, given = first_blend(
        activations, key_grads, momentum[0], basis, group, offsets, later
    )
    places = [0] * group
    arrived = [[] for _ in range(PARTS)]
    for i, offset in enumerate(offsets):
        places[offset] = i * block
        for p in range(PARTS):
            arrived[p].append(swap(given[i * PARTS + p], {"dp": offset}))
    for n, offset in enumerate(later):
        places[offset] = (len(offsets) + n) * block
        blended, given = blend(acts_later, held, basis, momentum_later[n], blended, n, places[offset])
        if offset == 0:
            own = list(given)
        else:
            for p in range(PARTS):
                arrived[p].append(swap(given[p], {"dp": offset}))
    sketches = [[None] * PARTS for _ in range(group)]
    for p in range(PARTS):
        for piece in arrived[p]:
            own[p] = own[p] + piece
        for mask in far:
            own[p] = own[p] + swap(own[p], {"dp": mask})
        own[p] = own[p] * (1.0 / n_dp)
        sketches[0][p] = own[p]
        for s in range(group - 1, 0, -1):
            sketches[s][p] = swap(own[p], {"dp": s})

    scale = 1.0 / n_dp
    pieces = [(places[0] + p * part, part) for p in range(PARTS)]
    *befores, held = right_terms(who, blended, pieces, own, scale, first=True)
    for p in range(PARTS):
        pieces = [(places[s] + p * part, part) for s in range(1, group)]
        given = [sketches[s][p] for s in range(1, group)]
        if p + 1 < PARTS:
            befores += right_terms(who, held, pieces, given, scale)
        else:
            keep, give, gram = right_terms(who, held, pieces, given, scale, befores)

    blocks = cut(who, keep, swap(give, {"rows": 1}), 1 << len(plane))
    gram = gram + swap(gram, {"rows": 1})
    row_masks = bits_of(n_rows)[1:]
    for mask in row_masks[:-1]:
        gram = gram + swap(gram, {"rows": mask})
    gram_other = swap(gram, {"rows": row_masks[-1]})
    right = blocks[0]
    for s in range(len(blocks) - 1, 0, -1):
        right = right + swap(blocks[s], masks_of([d for b, d in enumerate(plane) if s >> b & 1]))
    panels = list(range(0, rank, PANEL))
    middle = len(panels) // 2
    right, gram, gram_other = lax.optimization_barrier((right, gram, gram_other))
    state = None
    for step, mask in enumerate(bits_of(n_dp)[1:]):
        other = swap(right, {"dp": mask})
        if step == 0:
            state = factor(panels[:middle], gram, gram_other)
        elif step == 1:
            state = factor(panels[middle:], state)
        right, state = lax.optimization_barrier((right + other, state))
    flat = [sketches[s][p] for s in range(group) for p in range(PARTS)]
    ortho, own_ortho, held = orthonormal(who, state, flat, blended, group, n_dp)
    right, ortho = gather(right, plane, ortho)
    other = swap(right, {"rows": 1})

    new_momentum, new_basis, update = finish(
        who, right, other, state, ortho, own_ortho, held, places, n_rows,
        math.sqrt(local_rows * n_rows * kv / rank),
    )
    return (new_momentum[None], new_basis, update)


def solution(mesh):
    in_specs = (P("dp", "rows"), P("dp", None), P("dp", "rows", None), P())
    out_specs = (P("dp", "rows", None), P("rows", None), P(("rows", "dp"), None))
    return jax.shard_map(body, mesh=mesh, in_specs=in_specs, out_specs=out_specs, check_vma=False)
```

```python
import functools
import math

import jax
import jax.numpy as jnp
from jax import lax
from jax.experimental import pallas as pl
from jax.experimental.pallas import tpu as pltpu
from jax.sharding import PartitionSpec as P

MIB = 1024 * 1024
FIRST_MIB = 44
BLEND_MIB = 40
EXACT = lax.Precision.HIGHEST


def split(value):
    high = value.astype(jnp.bfloat16)
    return high, (value - high.astype(jnp.float32)).astype(jnp.bfloat16)


def dot(left, right, left_dim, right_dim, precision=None):
    return lax.dot_general(
        left,
        right,
        (((left_dim,), (right_dim,)), ((), ())),
        precision=precision,
        preferred_element_type=jnp.float32,
    )


def params(mib):
    return pltpu.CompilerParams(vmem_limit_bytes=mib * MIB)


def swap(value, masks):
    axes = tuple(a for a in ("dp", "rows") if a in masks)
    sizes = [lax.axis_size(a) for a in axes]
    pairs = []
    for index in range(math.prod(sizes)):
        rest, there = index, 0
        coords = []
        for size in sizes[::-1]:
            coords.append(rest % size)
            rest //= size
        for axis, size, coord in zip(axes, sizes, coords[::-1]):
            there = there * size + (coord ^ masks[axis])
        pairs.append((index, there))
    return lax.ppermute(value, axes, pairs)


def bits_of(count):
    return [1 << b for b in range(count.bit_length() - 1)]


def bit_set(axis, mask):
    return jnp.where((lax.axis_index(axis) & mask) != 0, 1, 0).astype(jnp.int32)


def masks_of(chosen):
    masks = {}
    for axis, mask in chosen:
        masks[axis] = masks.get(axis, 0) | mask
    return masks


def gather(value, directions, beside):
    count = 1 << len(directions)
    block = value.shape[0]
    mine = sum(bit_set(a, m) << b for b, (a, m) in enumerate(directions))
    parts = [value] + [
        swap(value, masks_of([d for b, d in enumerate(directions) if s >> b & 1])) for s in range(1, count)
    ]
    *parts, beside = lax.optimization_barrier((*parts, beside))
    out = jnp.zeros((count * block,) + value.shape[1:], value.dtype)
    for s, part in enumerate(parts):
        out = lax.dynamic_update_slice_in_dim(out, part, (mine ^ s) * block, 0)
    return out, beside


VMEM = pl.BlockSpec(memory_space=pltpu.VMEM)
ANY = pl.BlockSpec(memory_space=pl.ANY)
SMEM = pl.BlockSpec(memory_space=pltpu.SMEM)
PARTS = 2
CALLS = (((0, 0), (0, 1)), ((1, 0), (1, 1)))


def sketch_of(value, both, rank):
    high, low = split(value)
    wide = dot(high, both, 1, 0)
    return wide[:, :rank] + wide[:, rank:] + dot(low, both[:, :rank], 1, 0)


CHUNKS = 4


def first_blend_kernel(group, offsets, later, acts, grads, momentum, basis, *refs):
    count, extra = len(offsets), len(later)
    blended, held, acts_later = refs[:3]
    momentum_later = refs[3 : 3 + extra]
    sketches = refs[3 + extra : 3 + extra + PARTS * count]
    refs = refs[3 + extra + PARTS * count :]
    acts_held, values, both, acts_sem, grads_sem, momentum_sem, later_sem, out_sem = refs
    low = lax.axis_index("dp") & (group - 1)
    tokens, block = acts_held.shape[1:]
    rank = basis.shape[1]
    chunk = tokens // CHUNKS
    part = block // PARTS

    def start_of(offset):
        return pl.multiple_of((low ^ offset) * block, block)

    def acts_copy(i, c):
        here = pl.ds(c * chunk, chunk)
        return pltpu.make_async_copy(
            acts.at[here, pl.ds(start_of(offsets[i]), block)], acts_held.at[i, here], acts_sem.at[i, c]
        )

    def grads_copy(c):
        here = pl.ds(c * chunk, chunk)
        return pltpu.make_async_copy(grads.at[here], held.at[here], grads_sem.at[c])

    def momentum_copy(i):
        return pltpu.make_async_copy(
            momentum.at[pl.ds(start_of(offsets[i]), block)],
            values.at[pl.ds(i * block, block)],
            momentum_sem.at[i],
        )

    def out_copy(index):
        here = pl.ds(index * part, part)
        return pltpu.make_async_copy(values.at[here], blended.at[here], out_sem.at[index])

    def later_copies(i):
        here = pl.ds(start_of(later[i]), block)
        return [
            pltpu.make_async_copy(acts.at[:, here], acts_later.at[i], later_sem.at[i, 0]),
            pltpu.make_async_copy(momentum.at[here], momentum_later[i], later_sem.at[i, 1]),
        ]

    for c in range(CHUNKS):
        acts_copy(0, c).start()
        grads_copy(c).start()
    basis_high, basis_low = split(basis[...])
    both[:, :rank] = basis_high
    both[:, rank:] = basis_low
    columns = [slice(p * part, (p + 1) * part) for p in range(PARTS)]
    for i in range(count):
        if i == 0:
            sums = None
            for c in range(CHUNKS):
                acts_copy(0, c).wait()
                grads_copy(c).wait()
                if c == CHUNKS // 2:
                    momentum_copy(0).start()
                here = slice(c * chunk, (c + 1) * chunk)
                terms = [dot(acts_held[0, here, cols], held[here, :], 0, 0) for cols in columns]
                sums = terms if c == 0 else [a + b for a, b in zip(sums, terms)]
        else:
            for c in range(CHUNKS):
                acts_copy(i, c).wait()
        if i + 1 < count:
            for c in range(CHUNKS):
                acts_copy(i + 1, c).start()
            momentum_copy(i + 1).start()
        else:
            for n in range(extra):
                for copy in later_copies(n):
                    copy.start()
        momentum_copy(i).wait()
        for p, cols in enumerate(columns):
            rows = slice(i * block + p * part, i * block + (p + 1) * part)
            gradient = sums[p] if i == 0 else dot(acts_held[i, :, cols], held[...], 0, 0)
            values[rows, :] = values[rows, :] + gradient
            out_copy(i * PARTS + p).start()
        for index in range(i * PARTS, (i + 1) * PARTS):
            sketches[index][...] = sketch_of(values[index * part : (index + 1) * part, :], both[...], rank)
    for index in range(count * PARTS):
        out_copy(index).wait()
    for n in range(extra):
        for copy in later_copies(n):
            copy.wait()


def first_blend(acts, grads, momentum, basis, group, offsets, later):
    tokens, rows = acts.shape
    kv, rank = basis.shape
    block = rows // group
    count, extra = len(offsets), len(later)
    outs = [
        jax.ShapeDtypeStruct((rows, kv), jnp.float32),
        pltpu.VMEM((tokens, kv), jnp.bfloat16),
        pltpu.VMEM((extra, tokens, block), jnp.bfloat16),
    ]
    outs += [pltpu.VMEM((block, kv), jnp.float32)] * extra
    outs += [pltpu.VMEM((block // PARTS, rank), jnp.float32)] * (PARTS * count)
    out = pl.pallas_call(
        functools.partial(first_blend_kernel, group, offsets, later),
        in_specs=[ANY, ANY, ANY, VMEM],
        out_specs=[ANY] + [VMEM] * (len(outs) - 1),
        out_shape=outs,
        scratch_shapes=[
            pltpu.VMEM((count, tokens, block), jnp.bfloat16),
            pltpu.VMEM((count * block, kv), jnp.float32),
            pltpu.VMEM((kv, 2 * rank), jnp.bfloat16),
            pltpu.SemaphoreType.DMA((count, CHUNKS)),
            pltpu.SemaphoreType.DMA((CHUNKS,)),
            pltpu.SemaphoreType.DMA((count,)),
            pltpu.SemaphoreType.DMA((extra, 2)),
            pltpu.SemaphoreType.DMA((count * PARTS,)),
        ],
        compiler_params=params(FIRST_MIB),
        name="first_blend",
    )(acts, grads, momentum, basis)
    return out[0], out[1], out[2], out[3 : 3 + extra], out[3 + extra :]


def blend_kernel(jobs, extra, acts, grads, basis, *refs):
    momentum, refs = refs[:extra], refs[extra + 1 :]
    blended, sketches, (values, out_sem) = refs[0], refs[1:-2], refs[-2:]
    rank = basis.shape[1]
    part = values.shape[0] // len(jobs)
    both = jnp.concatenate(split(basis[...]), 1)
    copies = []
    for n, (which, p, place) in enumerate(jobs):
        here = slice(n * part, (n + 1) * part)
        rows = slice(p * part, (p + 1) * part)
        values[here, :] = momentum[which][rows, :] + dot(acts[which, :, rows], grads[...], 0, 0)
        copies.append(
            pltpu.make_async_copy(values.at[here], blended.at[pl.ds(place + p * part, part)], out_sem.at[n])
        )
        copies[-1].start()
    for n, sketch in enumerate(sketches):
        sketch[...] = sketch_of(values[n * part : (n + 1) * part, :], both, rank)
    for copy in copies:
        copy.wait()


def blend(acts, grads, basis, momentum, blended, jobs):
    block = acts.shape[2]
    kv, rank = basis.shape
    part = block // PARTS
    outs = [jax.ShapeDtypeStruct(blended.shape, jnp.float32)]
    outs += [pltpu.VMEM((part, rank), jnp.float32)] * len(jobs)
    out = pl.pallas_call(
        functools.partial(blend_kernel, jobs, len(momentum)),
        in_specs=[VMEM] * (3 + len(momentum)) + [ANY],
        out_specs=[ANY] + [VMEM] * len(jobs),
        out_shape=outs,
        scratch_shapes=[
            pltpu.VMEM((len(jobs) * part, kv), jnp.float32),
            pltpu.SemaphoreType.DMA((len(jobs),)),
        ],
        input_output_aliases={3 + len(momentum): 0},
        compiler_params=params(BLEND_MIB),
        name="blend",
    )(acts, grads, basis, *momentum, blended)
    return out[0], out[1:]


def right_product(sketch, blended):
    turned = sketch.T
    rank = turned.shape[0]
    high, low = split(turned)
    stacked = jnp.concatenate([high, low], 0)
    blended_high, blended_low = split(blended)
    wide = dot(stacked, blended_high, 1, 0)
    gram = dot(stacked, stacked, 1, 1)
    gram = gram[:rank, :rank] + gram[rank:, rank:] + (gram[:rank, rank:] + gram[rank:, :rank])
    return wide[:rank] + wide[rank:] + dot(high, blended_low, 1, 0), gram


def pack(gram, width):
    rank = gram.shape[0]
    rows = rank * rank // width
    return jnp.concatenate([gram[k * rows : (k + 1) * rows, :] for k in range(rank // rows)], 1)


def unpack(packed, rank):
    return jnp.concatenate([packed[:, k * rank : (k + 1) * rank] for k in range(packed.shape[1] // rank)], 0)


def right_kernel(pieces, first, last, scale, *refs):
    who, blended = refs[:2]
    refs = refs[2:]
    sketches, refs = refs[: len(pieces)], refs[len(pieces) :]
    if first:
        held, sem = refs[-2:]
        start, rows = pieces[0][0], sum(r for _, r in pieces)
        copies = []
        for at, size in ((start, rows), (0, start), (start + rows, blended.shape[0] - start - rows)):
            if size:
                here = pl.ds(at, size)
                copies.append(pltpu.make_async_copy(blended.at[here], held.at[here], sem.at[len(copies)]))
                copies[-1].start()
        copies[0].wait()
        blended = held
    right, gram = None, None
    for (start, rows), sketch in zip(pieces, sketches):
        right_term, gram_term = right_product(sketch[...], blended[start : start + rows, :])
        right = right_term if right is None else right + right_term
        gram = gram_term if gram is None else gram + gram_term
    right = scale * right
    if not last:
        refs[0][...] = right
        refs[1][...] = gram
        if first:
            for copy in copies[1:]:
                copy.wait()
        return
    befores, refs = refs[:-3], refs[-3:]
    keep, give, total = refs
    for before in befores[::2]:
        right = right + before[...]
    for before in befores[1::2]:
        gram = gram + before[...]
    total[...] = right
    half = total.shape[0] // 2
    core = who[2] & 1
    keep[:half, :] = total[pl.ds(pl.multiple_of(core * half, half), half), :]
    give[:half, :] = total[pl.ds(pl.multiple_of((1 - core) * half, half), half), :]
    packed = pack(gram, right.shape[1])
    keep[half:, :] = packed
    give[half:, :] = packed


def right_terms(who, blended, pieces, sketches, scale, befores=None, first=False):
    rank = sketches[0].shape[1]
    kv = blended.shape[1]
    last = befores is not None
    gram = pltpu.VMEM((rank, rank), jnp.float32)
    if last:
        outs = [pltpu.VMEM((rank // 2 + rank * rank // kv, kv), jnp.float32)] * 2
    else:
        outs = [pltpu.VMEM((rank, kv), jnp.float32), pltpu.VMEM((rank, rank), jnp.float32)]
    scratch = [pltpu.VMEM((rank, kv), jnp.float32)] if last else []
    if first:
        outs.append(pltpu.VMEM(blended.shape, jnp.float32))
        scratch = [pltpu.SemaphoreType.DMA((3,))]
    operands = [who, blended, *sketches, *(befores or [])]
    return pl.pallas_call(
        functools.partial(right_kernel, pieces, first, last, scale),
        in_specs=[SMEM, ANY if first else VMEM] + [VMEM] * (len(operands) - 2),
        out_specs=[VMEM] * len(outs),
        out_shape=outs,
        scratch_shapes=scratch,
        compiler_params=params(FIRST_MIB if first else 16),
        name="right_terms",
    )(*operands)


def cut_kernel(count, who, keep, arrived, *outs):
    blocks, gram = outs[:-1], outs[-1]
    block = blocks[0].shape[0]
    half = count * block
    packed = keep[half:, :] + arrived[half:, :]
    gram[...] = packed
    for s, out in enumerate(blocks):
        here = pl.ds(pl.multiple_of((who[3] ^ s) * block, block), block)
        out[:block, :] = keep[here, :] + arrived[here, :]
        if 0 < s < count // 2:
            out[block:, :] = packed


def cut(who, keep, arrived, rank, count):
    kv = keep.shape[1]
    block = rank // 2 // count
    extra = rank * rank // kv
    shapes = [(block + (extra if 0 < s < count // 2 else 0), kv) for s in range(count)] + [(extra, kv)]
    return pl.pallas_call(
        functools.partial(cut_kernel, count),
        in_specs=[SMEM, VMEM, VMEM],
        out_specs=[VMEM] * len(shapes),
        out_shape=[pltpu.VMEM(shape, jnp.float32) for shape in shapes],
        compiler_params=params(16),
        name="cut",
    )(who, keep, arrived)


PANEL = 16


def factor_kernel(panels, grams, block, *refs):
    out = refs[-1]
    rank = out.shape[0]
    if grams:
        packed = refs[0][...]
        for ref in refs[1:grams]:
            packed = packed + ref[block:, :]
        rows_id = lax.broadcasted_iota(jnp.int32, (rank, rank), 0)
        cols_id = lax.broadcasted_iota(jnp.int32, (rank, rank), 1)
        out[:, :rank] = unpack(packed, rank)
        out[:, rank:] = jnp.where(rows_id == cols_id, 1.0, 0.0)
    else:
        out[...] = refs[0][...]
    index = lax.broadcasted_iota(jnp.int32, (PANEL, rank), 0)
    for start in panels:
        here = slice(start, start + PANEL)
        left = out[here, :rank]
        right = out[here, rank:]
        columns = [
            jnp.broadcast_to(left[:, start + c : start + c + 1], (PANEL, rank)) for c in range(PANEL)
        ]
        pivots = jnp.ones((PANEL, rank), jnp.float32)
        for j in range(PANEL):
            pivot = columns[j][j : j + 1, :]
            pivots = jnp.where(index == j, pivot, pivots)
            factor = jnp.where(index > j, columns[j] * (1.0 / pivot), 0.0)
            for c in range(j + 1, PANEL):
                columns[c] = columns[c] - factor * columns[c][j : j + 1, :]
            left = left - factor * left[j : j + 1, :]
            right = right - factor * right[j : j + 1, :]
        weight = 1.0 / jnp.sqrt(pivots)
        left = left * weight
        right = right * weight
        out[here, :rank] = left
        out[here, rank:] = right
        if start + PANEL < rank:
            rows = jnp.concatenate([left, right], 1)
            high, rest = split(rows)
            middle = rest
            low = (rows - high.astype(jnp.float32) - middle.astype(jnp.float32)).astype(jnp.bfloat16)
            one = jnp.concatenate([high, high, middle, middle, high, low], 0)[:, :rank]
            two = jnp.concatenate([high, middle, high, middle, low, high], 0)
            update = dot(one, two, 0, 0)
            below = slice(start + PANEL, rank)
            out[below, :] = out[below, :] - update[start + PANEL :, :]


def factor(panels, rank, inputs, grams, block):
    return pl.pallas_call(
        functools.partial(factor_kernel, panels, grams, block),
        in_specs=[VMEM] * len(inputs),
        out_specs=VMEM,
        out_shape=pltpu.VMEM((rank, 2 * rank), jnp.float32),
        compiler_params=params(16),
        name="factor",
    )(*inputs)


LOADS = 4


def load_kernel(source, token, held, sem):
    rows = source.shape[0] // LOADS
    copies = []
    for n in range(LOADS):
        here = pl.ds(n * rows, rows)
        copies.append(pltpu.make_async_copy(source.at[here], held.at[here], sem.at[n]))
        copies[-1].start()
    for copy in copies:
        copy.wait()


def load(source, token):
    return pl.pallas_call(
        load_kernel,
        in_specs=[ANY, ANY],
        out_specs=VMEM,
        out_shape=pltpu.VMEM(source.shape, source.dtype),
        scratch_shapes=[pltpu.SemaphoreType.DMA((LOADS,))],
        compiler_params=params(FIRST_MIB),
        name="load",
    )(source, token)


def ortho_kernel(group, who, state, *refs):
    sketches, refs = refs[: PARTS * group], refs[PARTS * group :]
    ortho, own_ortho, total = refs
    rank = state.shape[0]
    part = sketches[0].shape[0]
    inverse = state[:, rank:]
    for s in range(group):
        for p in range(PARTS):
            value = sketches[s * PARTS + p][...]
            high, low = split(value)
            first, second = split(inverse)
            wide = dot(high, jnp.concatenate([first, second], 0), 1, 1)
            value = wide[:, :rank] + wide[:, rank:] + dot(low, first, 1, 1)
            rows = slice((s * PARTS + p) * part, (s * PARTS + p + 1) * part)
            ortho[rows, :] = jnp.concatenate(split(value), 1)
            start = ((who[0] ^ s) * PARTS + p) * part
            total[pl.ds(pl.multiple_of(start, part), part), :] = value
    own = own_ortho.shape[0]
    own_ortho[...] = total[pl.ds(pl.multiple_of(who[1] * own, own), own), :]


def orthonormal(who, state, sketches, group, n_dp):
    rank = state.shape[0]
    rows = sketches[0].shape[0] * len(sketches)
    return pl.pallas_call(
        functools.partial(ortho_kernel, group),
        in_specs=[SMEM] + [VMEM] * (1 + len(sketches)),
        out_specs=[VMEM] * 2,
        out_shape=[
            pltpu.VMEM((rows, 2 * rank), jnp.bfloat16),
            pltpu.VMEM((rows // n_dp, rank), jnp.float32),
        ],
        scratch_shapes=[pltpu.VMEM((rows, rank), jnp.float32)],
        compiler_params=params(16),
        name="ortho",
    )(who, state, *sketches)


CUTS = 2


def finish_kernel(group, places, scale, who, right_here, right_there, state, ortho, own_ortho, *refs):
    blended, new_momentum, new_basis, update, right, values, coeff_high, coeff_low, sem = refs
    rank, kv = right.shape
    half = rank // 2
    core = who[2] & 1
    right[pl.ds(pl.multiple_of(core * half, half), half), :] = right_here[...]
    right[pl.ds(pl.multiple_of((1 - core) * half, half), half), :] = right_there[...]
    coeff = dot(state[:, rank:], right[...], 1, 0, EXACT)
    high, low = split(0.2 * coeff)
    coeff_high[:rank, :] = high
    coeff_high[rank:, :] = high
    coeff_low[...] = low
    block = values.shape[0] // group
    rows = block // CUTS
    copies = []
    for s in range(group):
        for c in range(CUTS):
            here = slice(s * block + c * rows, s * block + (c + 1) * rows)
            part = ortho[here, :]
            feedback = dot(part, coeff_high[...], 1, 0) + dot(part[:, :rank], coeff_low[...], 1, 0)
            at = places[s] + c * rows
            values[here, :] = blended[at : at + rows, :] - feedback
            there = pl.multiple_of((who[0] ^ s) * block + c * rows, rows)
            copies.append(
                pltpu.make_async_copy(values.at[here], new_momentum.at[pl.ds(there, rows)], sem.at[len(copies)])
            )
            copies[-1].start()
    norm = jnp.sqrt(jnp.sum(coeff * coeff, axis=1, keepdims=True) + 1e-06)
    normed = coeff / norm
    count = new_basis.shape[0]
    for j in range(kv // count):

        @pl.when(who[2] == j)
        def _(j=j):
            new_basis[...] = normed[:, j * count : (j + 1) * count].T

    rows_high, rows_low = split(own_ortho[...])
    high, low = split(normed)
    product = dot(jnp.concatenate([rows_high, rows_low], 1), jnp.concatenate([high, high], 0), 1, 0)
    update[...] = (scale * (product + dot(rows_high, low, 1, 0))).astype(update.dtype)
    for copy in copies:
        copy.wait()


def finish(who, right_here, right_there, state, ortho, own_ortho, blended, places, n_rows, scale):
    rank, kv = 2 * right_here.shape[0], right_here.shape[1]
    group = len(places)
    rows = ortho.shape[0]
    return pl.pallas_call(
        functools.partial(finish_kernel, group, places, scale),
        in_specs=[SMEM] + [VMEM] * 6,
        out_specs=[ANY, VMEM, VMEM],
        out_shape=[
            jax.ShapeDtypeStruct((rows, kv), jnp.float32),
            jax.ShapeDtypeStruct((kv // n_rows, rank), jnp.float32),
            jax.ShapeDtypeStruct(own_ortho.shape[:1] + (kv,), jnp.bfloat16),
        ],
        scratch_shapes=[
            pltpu.VMEM((rank, kv), jnp.float32),
            pltpu.VMEM((rows, kv), jnp.float32),
            pltpu.VMEM((2 * rank, kv), jnp.bfloat16),
            pltpu.VMEM((rank, kv), jnp.bfloat16),
            pltpu.SemaphoreType.DMA((group * CUTS,)),
        ],
        compiler_params=params(32),
        name="finish",
    )(who, right_here, right_there, state, ortho, own_ortho, blended)


def body(activations, key_grads, momentum, basis):
    n_dp = lax.axis_size("dp")
    n_rows = lax.axis_size("rows")
    dp = lax.axis_index("dp")
    group = min(4, n_dp)
    low = dp & (group - 1)
    kv, rank = basis.shape
    local_rows = activations.shape[1]
    block = local_rows // group
    part = block // PARTS
    far = [mask for mask in bits_of(n_dp) if mask >= group]
    plane = [("rows", m) for m in bits_of(n_rows)[1:]] + [("dp", 1)]
    mine = sum(bit_set(a, m) << b for b, (a, m) in enumerate(plane))
    who = jnp.stack([low, dp, lax.axis_index("rows"), mine]).astype(jnp.int32)

    offsets, later = tuple(range(group - 1, 1, -1)), (1, 0)
    blended, held, acts_later, momentum_later, given = first_blend(
        activations, key_grads, momentum[0], basis, group, offsets, later
    )
    places = [0] * group
    arrived = [[] for _ in range(PARTS)]
    for i, offset in enumerate(offsets):
        places[offset] = i * block
        for p in range(PARTS):
            arrived[p].append(swap(given[i * PARTS + p], {"dp": offset}))
    for n, offset in enumerate(later):
        places[offset] = (len(offsets) + n) * block
    own = [None] * PARTS
    for calls in CALLS:
        jobs = tuple((n, p, places[later[n]]) for n, p in calls)
        blended, given = blend(acts_later, held, basis, momentum_later, blended, jobs)
        for (n, p), value in zip(calls, given):
            if later[n] == 0:
                own[p] = value
            else:
                arrived[p].append(swap(value, {"dp": later[n]}))
    sketches = [[None] * PARTS for _ in range(group)]
    for p in range(PARTS):
        for piece in arrived[p]:
            own[p] = own[p] + piece
        for mask in far:
            own[p] = own[p] + swap(own[p], {"dp": mask})
        own[p] = own[p] * (1.0 / n_dp)
        sketches[0][p] = own[p]
        for s in range(group - 1, 0, -1):
            sketches[s][p] = swap(own[p], {"dp": s})

    scale = 1.0 / n_dp
    pieces = [(places[0] + p * part, part) for p in range(PARTS)]
    *befores, held = right_terms(who, blended, pieces, own, scale, first=True)
    for p in range(PARTS):
        pieces = [(places[s] + p * part, part) for s in range(1, group)]
        given = [sketches[s][p] for s in range(1, group)]
        if p + 1 < PARTS:
            befores += right_terms(who, held, pieces, given, scale)
        else:
            keep, give = right_terms(who, held, pieces, given, scale, befores)

    count = 1 << len(plane)
    *blocks, gram = cut(who, keep, swap(give, {"rows": 1}), rank, count)
    right = blocks[0]
    block = right.shape[0]
    grams = [gram]
    for s in range(count - 1, 0, -1):
        piece = swap(blocks[s], masks_of([d for b, d in enumerate(plane) if s >> b & 1]))
        if s < count // 2:
            grams.append(piece)
            piece = piece[:block]
        right = right + piece
    panels = list(range(0, rank, PANEL))
    middle = len(panels) // 2
    state = factor(panels, rank, grams, len(grams), block)
    masks = bits_of(n_dp)[1:]
    for first in range(0, len(masks), 2):
        pair = masks[first : first + 2]
        pieces = [swap(right, {"dp": mask}) for mask in ([sum(pair)] + pair[::-1])[: 2 ** len(pair) - 1]]
        *pieces, state = lax.optimization_barrier((*pieces, state))
        for piece in pieces:
            right = right + piece
    flat = [sketches[s][p] for s in range(group) for p in range(PARTS)]
    right, held = gather(right, plane, load(blended, right))
    other = swap(right, {"rows": 1})
    ortho, own_ortho = orthonormal(who, state, flat, group, n_dp)

    new_momentum, new_basis, update = finish(
        who, right, other, state, ortho, own_ortho, held, places, n_rows,
        math.sqrt(local_rows * n_rows * kv / rank),
    )
    return (new_momentum[None], new_basis, update)


def solution(mesh):
    in_specs = (P("dp", "rows"), P("dp", None), P("dp", "rows", None), P())
    out_specs = (P("dp", "rows", None), P("rows", None), P(("rows", "dp"), None))
    return jax.shard_map(body, mesh=mesh, in_specs=in_specs, out_specs=out_specs, check_vma=False)
```

```python
import functools
import math

import jax
import jax.numpy as jnp
from jax import lax
from jax.experimental import pallas as pl
from jax.experimental.pallas import tpu as pltpu
from jax.sharding import PartitionSpec as P

MIB = 1024 * 1024
FIRST_MIB = 44
BLEND_MIB = 40
EXACT = lax.Precision.HIGHEST


def split(value):
    high = value.astype(jnp.bfloat16)
    return high, (value - high.astype(jnp.float32)).astype(jnp.bfloat16)


def dot(left, right, left_dim, right_dim, precision=None):
    return lax.dot_general(
        left,
        right,
        (((left_dim,), (right_dim,)), ((), ())),
        precision=precision,
        preferred_element_type=jnp.float32,
    )


def params(mib):
    return pltpu.CompilerParams(vmem_limit_bytes=mib * MIB)


def swap(value, masks):
    axes = tuple(a for a in ("dp", "rows") if a in masks)
    sizes = [lax.axis_size(a) for a in axes]
    pairs = []
    for index in range(math.prod(sizes)):
        rest, there = index, 0
        coords = []
        for size in sizes[::-1]:
            coords.append(rest % size)
            rest //= size
        for axis, size, coord in zip(axes, sizes, coords[::-1]):
            there = there * size + (coord ^ masks[axis])
        pairs.append((index, there))
    return lax.ppermute(value, axes, pairs)


def bits_of(count):
    return [1 << b for b in range(count.bit_length() - 1)]


def bit_set(axis, mask):
    return jnp.where((lax.axis_index(axis) & mask) != 0, 1, 0).astype(jnp.int32)


def masks_of(chosen):
    masks = {}
    for axis, mask in chosen:
        masks[axis] = masks.get(axis, 0) | mask
    return masks


def gather(value, directions, beside):
    count = 1 << len(directions)
    block = value.shape[0]
    mine = sum(bit_set(a, m) << b for b, (a, m) in enumerate(directions))
    parts = [value] + [
        swap(value, masks_of([d for b, d in enumerate(directions) if s >> b & 1])) for s in range(1, count)
    ]
    *parts, beside = lax.optimization_barrier((*parts, beside))
    out = jnp.zeros((count * block,) + value.shape[1:], value.dtype)
    for s, part in enumerate(parts):
        out = lax.dynamic_update_slice_in_dim(out, part, (mine ^ s) * block, 0)
    return out, beside


VMEM = pl.BlockSpec(memory_space=pltpu.VMEM)
ANY = pl.BlockSpec(memory_space=pl.ANY)
SMEM = pl.BlockSpec(memory_space=pltpu.SMEM)
PARTS = 2
CALLS = (((0, 0), (0, 1)), ((1, 0), (1, 1)))


def sketch_of(value, both, rank):
    high, low = split(value)
    wide = dot(high, both, 1, 0)
    return wide[:, :rank] + wide[:, rank:] + dot(low, both[:, :rank], 1, 0)


CHUNKS = 2


def first_blend_kernel(group, offsets, later, acts, grads, momentum, basis, *refs):
    count, extra = len(offsets), len(later)
    blended, held, acts_later = refs[:3]
    momentum_later = refs[3 : 3 + extra]
    sketches = refs[3 + extra : 3 + extra + PARTS * count]
    refs = refs[3 + extra + PARTS * count :]
    acts_held, values, basis_held, both, acts_sem, grads_sem, momentum_sem, later_sem, out_sem, basis_sem = refs
    low = lax.axis_index("dp") & (group - 1)
    tokens, block = acts_held.shape[1:]
    rank = basis.shape[1]
    chunk = tokens // CHUNKS
    part = block // PARTS

    def start_of(offset):
        return pl.multiple_of((low ^ offset) * block, block)

    def acts_copy(i, c):
        here = pl.ds(c * chunk, chunk)
        return pltpu.make_async_copy(
            acts.at[here, pl.ds(start_of(offsets[i]), block)], acts_held.at[i, here], acts_sem.at[i, c]
        )

    def grads_copy(c):
        here = pl.ds(c * chunk, chunk)
        return pltpu.make_async_copy(grads.at[here], held.at[here], grads_sem.at[c])

    def momentum_copy(i):
        return pltpu.make_async_copy(
            momentum.at[pl.ds(start_of(offsets[i]), block)],
            values.at[pl.ds(i * block, block)],
            momentum_sem.at[i],
        )

    def out_copy(index):
        here = pl.ds(index * part, part)
        return pltpu.make_async_copy(values.at[here], blended.at[here], out_sem.at[index])

    def later_copies(i):
        here = pl.ds(start_of(later[i]), block)
        return [
            pltpu.make_async_copy(acts.at[:, here], acts_later.at[i], later_sem.at[i, 0]),
            pltpu.make_async_copy(momentum.at[here], momentum_later[i], later_sem.at[i, 1]),
        ]

    for c in range(CHUNKS):
        acts_copy(0, c).start()
        grads_copy(c).start()
    basis_copy = pltpu.make_async_copy(basis, basis_held, basis_sem)
    basis_copy.start()
    columns = [slice(p * part, (p + 1) * part) for p in range(PARTS)]
    for i in range(count):
        if i == 0:
            sums = None
            for c in range(CHUNKS):
                acts_copy(0, c).wait()
                grads_copy(c).wait()
                if c == CHUNKS // 2:
                    momentum_copy(0).start()
                here = slice(c * chunk, (c + 1) * chunk)
                terms = [dot(acts_held[0, here, cols], held[here, :], 0, 0) for cols in columns]
                sums = terms if c == 0 else [a + b for a, b in zip(sums, terms)]
        else:
            for c in range(CHUNKS):
                acts_copy(i, c).wait()
        if i + 1 < count:
            for c in range(CHUNKS):
                acts_copy(i + 1, c).start()
            momentum_copy(i + 1).start()
        else:
            for n in range(extra):
                for copy in later_copies(n):
                    copy.start()
        momentum_copy(i).wait()
        for p, cols in enumerate(columns):
            rows = slice(i * block + p * part, i * block + (p + 1) * part)
            gradient = sums[p] if i == 0 else dot(acts_held[i, :, cols], held[...], 0, 0)
            values[rows, :] = values[rows, :] + gradient
            out_copy(i * PARTS + p).start()
        if i == 0:
            basis_copy.wait()
            basis_high, basis_low = split(basis_held[...])
            both[:, :rank] = basis_high
            both[:, rank:] = basis_low
        for index in range(i * PARTS, (i + 1) * PARTS):
            sketches[index][...] = sketch_of(values[index * part : (index + 1) * part, :], both[...], rank)
    for index in range(count * PARTS):
        out_copy(index).wait()
    for n in range(extra):
        for copy in later_copies(n):
            copy.wait()


def first_blend(acts, grads, momentum, basis, group, offsets, later):
    tokens, rows = acts.shape
    kv, rank = basis.shape
    block = rows // group
    count, extra = len(offsets), len(later)
    outs = [
        jax.ShapeDtypeStruct((rows, kv), jnp.float32),
        pltpu.VMEM((tokens, kv), jnp.bfloat16),
        pltpu.VMEM((extra, tokens, block), jnp.bfloat16),
    ]
    outs += [pltpu.VMEM((block, kv), jnp.float32)] * extra
    outs += [pltpu.VMEM((block // PARTS, rank), jnp.float32)] * (PARTS * count)
    out = pl.pallas_call(
        functools.partial(first_blend_kernel, group, offsets, later),
        in_specs=[ANY, ANY, ANY, ANY],
        out_specs=[ANY] + [VMEM] * (len(outs) - 1),
        out_shape=outs,
        scratch_shapes=[
            pltpu.VMEM((count, tokens, block), jnp.bfloat16),
            pltpu.VMEM((count * block, kv), jnp.float32),
            pltpu.VMEM((kv, rank), jnp.float32),
            pltpu.VMEM((kv, 2 * rank), jnp.bfloat16),
            pltpu.SemaphoreType.DMA((count, CHUNKS)),
            pltpu.SemaphoreType.DMA((CHUNKS,)),
            pltpu.SemaphoreType.DMA((count,)),
            pltpu.SemaphoreType.DMA((extra, 2)),
            pltpu.SemaphoreType.DMA((count * PARTS,)),
            pltpu.SemaphoreType.DMA,
        ],
        compiler_params=params(FIRST_MIB),
        name="first_blend",
    )(acts, grads, momentum, basis)
    return out[0], out[1], out[2], out[3 : 3 + extra], out[3 + extra :]


def blend_kernel(jobs, extra, acts, grads, basis, *refs):
    momentum, refs = refs[:extra], refs[extra + 1 :]
    blended, sketches, (values, out_sem) = refs[0], refs[1:-2], refs[-2:]
    rank = basis.shape[1]
    part = values.shape[0] // len(jobs)
    both = jnp.concatenate(split(basis[...]), 1)
    copies = []
    for n, (which, p, place) in enumerate(jobs):
        here = slice(n * part, (n + 1) * part)
        rows = slice(p * part, (p + 1) * part)
        values[here, :] = momentum[which][rows, :] + dot(acts[which, :, rows], grads[...], 0, 0)
        copies.append(
            pltpu.make_async_copy(values.at[here], blended.at[pl.ds(place + p * part, part)], out_sem.at[n])
        )
        copies[-1].start()
    for n, sketch in enumerate(sketches):
        sketch[...] = sketch_of(values[n * part : (n + 1) * part, :], both, rank)
    for copy in copies:
        copy.wait()


def blend(acts, grads, basis, momentum, blended, jobs):
    block = acts.shape[2]
    kv, rank = basis.shape
    part = block // PARTS
    outs = [jax.ShapeDtypeStruct(blended.shape, jnp.float32)]
    outs += [pltpu.VMEM((part, rank), jnp.float32)] * len(jobs)
    out = pl.pallas_call(
        functools.partial(blend_kernel, jobs, len(momentum)),
        in_specs=[VMEM] * (3 + len(momentum)) + [ANY],
        out_specs=[ANY] + [VMEM] * len(jobs),
        out_shape=outs,
        scratch_shapes=[
            pltpu.VMEM((len(jobs) * part, kv), jnp.float32),
            pltpu.SemaphoreType.DMA((len(jobs),)),
        ],
        input_output_aliases={3 + len(momentum): 0},
        compiler_params=params(BLEND_MIB),
        name="blend",
    )(acts, grads, basis, *momentum, blended)
    return out[0], out[1:]


def right_product(sketch, blended):
    turned = sketch.T
    rank = turned.shape[0]
    high, low = split(turned)
    stacked = jnp.concatenate([high, low], 0)
    blended_high, blended_low = split(blended)
    wide = dot(stacked, blended_high, 1, 0)
    gram = dot(stacked, stacked, 1, 1)
    gram = gram[:rank, :rank] + gram[rank:, rank:] + (gram[:rank, rank:] + gram[rank:, :rank])
    return wide[:rank] + wide[rank:] + dot(high, blended_low, 1, 0), gram


def pack(gram, width):
    rank = gram.shape[0]
    rows = rank * rank // width
    return jnp.concatenate([gram[k * rows : (k + 1) * rows, :] for k in range(rank // rows)], 1)


def unpack(packed, rank):
    return jnp.concatenate([packed[:, k * rank : (k + 1) * rank] for k in range(packed.shape[1] // rank)], 0)


def right_kernel(pieces, first, last, scale, *refs):
    who, blended = refs[:2]
    refs = refs[2:]
    sketches, refs = refs[: len(pieces)], refs[len(pieces) :]
    if first:
        held, sem = refs[-2:]
        start, rows = pieces[0][0], sum(r for _, r in pieces)
        copies = []
        for at, size in ((start, rows), (0, start), (start + rows, blended.shape[0] - start - rows)):
            if size:
                here = pl.ds(at, size)
                copies.append(pltpu.make_async_copy(blended.at[here], held.at[here], sem.at[len(copies)]))
                copies[-1].start()
        copies[0].wait()
        blended = held
    right, gram = None, None
    for (start, rows), sketch in zip(pieces, sketches):
        right_term, gram_term = right_product(sketch[...], blended[start : start + rows, :])
        right = right_term if right is None else right + right_term
        gram = gram_term if gram is None else gram + gram_term
    right = scale * right
    if not last:
        refs[0][...] = right
        refs[1][...] = gram
        if first:
            for copy in copies[1:]:
                copy.wait()
        return
    befores, refs = refs[:-3], refs[-3:]
    keep, give, total = refs
    for before in befores[::2]:
        right = right + before[...]
    for before in befores[1::2]:
        gram = gram + before[...]
    total[...] = right
    half = total.shape[0] // 2
    core = who[2] & 1
    keep[:half, :] = total[pl.ds(pl.multiple_of(core * half, half), half), :]
    give[:half, :] = total[pl.ds(pl.multiple_of((1 - core) * half, half), half), :]
    packed = pack(gram, right.shape[1])
    keep[half:, :] = packed
    give[half:, :] = packed


def right_terms(who, blended, pieces, sketches, scale, befores=None, first=False):
    rank = sketches[0].shape[1]
    kv = blended.shape[1]
    last = befores is not None
    gram = pltpu.VMEM((rank, rank), jnp.float32)
    if last:
        outs = [pltpu.VMEM((rank // 2 + rank * rank // kv, kv), jnp.float32)] * 2
    else:
        outs = [pltpu.VMEM((rank, kv), jnp.float32), pltpu.VMEM((rank, rank), jnp.float32)]
    scratch = [pltpu.VMEM((rank, kv), jnp.float32)] if last else []
    if first:
        outs.append(pltpu.VMEM(blended.shape, jnp.float32))
        scratch = [pltpu.SemaphoreType.DMA((3,))]
    operands = [who, blended, *sketches, *(befores or [])]
    return pl.pallas_call(
        functools.partial(right_kernel, pieces, first, last, scale),
        in_specs=[SMEM, ANY if first else VMEM] + [VMEM] * (len(operands) - 2),
        out_specs=[VMEM] * len(outs),
        out_shape=outs,
        scratch_shapes=scratch,
        compiler_params=params(FIRST_MIB if first else 16),
        name="right_terms",
    )(*operands)


def cut_kernel(count, who, keep, arrived, *outs):
    blocks, gram = outs[:-1], outs[-1]
    block = blocks[0].shape[0]
    half = count * block
    packed = keep[half:, :] + arrived[half:, :]
    gram[...] = packed
    for s, out in enumerate(blocks):
        here = pl.ds(pl.multiple_of((who[3] ^ s) * block, block), block)
        out[:block, :] = keep[here, :] + arrived[here, :]
        if 0 < s < count // 2:
            out[block:, :] = packed


def cut(who, keep, arrived, rank, count):
    kv = keep.shape[1]
    block = rank // 2 // count
    extra = rank * rank // kv
    shapes = [(block + (extra if 0 < s < count // 2 else 0), kv) for s in range(count)] + [(extra, kv)]
    return pl.pallas_call(
        functools.partial(cut_kernel, count),
        in_specs=[SMEM, VMEM, VMEM],
        out_specs=[VMEM] * len(shapes),
        out_shape=[pltpu.VMEM(shape, jnp.float32) for shape in shapes],
        compiler_params=params(16),
        name="cut",
    )(who, keep, arrived)


PANEL = 16


def factor_kernel(panels, grams, block, *refs):
    out = refs[-1]
    rank = out.shape[0]
    if grams:
        packed = refs[0][...]
        for ref in refs[1:grams]:
            packed = packed + ref[block:, :]
        rows_id = lax.broadcasted_iota(jnp.int32, (rank, rank), 0)
        cols_id = lax.broadcasted_iota(jnp.int32, (rank, rank), 1)
        out[:, :rank] = unpack(packed, rank)
        out[:, rank:] = jnp.where(rows_id == cols_id, 1.0, 0.0)
    else:
        out[...] = refs[0][...]
    index = lax.broadcasted_iota(jnp.int32, (PANEL, rank), 0)
    for start in panels:
        here = slice(start, start + PANEL)
        left = out[here, :rank]
        right = out[here, rank:]
        columns = [
            jnp.broadcast_to(left[:, start + c : start + c + 1], (PANEL, rank)) for c in range(PANEL)
        ]
        pivots = jnp.ones((PANEL, rank), jnp.float32)
        for j in range(PANEL):
            pivot = columns[j][j : j + 1, :]
            pivots = jnp.where(index == j, pivot, pivots)
            factor = jnp.where(index > j, columns[j] * (1.0 / pivot), 0.0)
            for c in range(j + 1, PANEL):
                columns[c] = columns[c] - factor * columns[c][j : j + 1, :]
            left = left - factor * left[j : j + 1, :]
            right = right - factor * right[j : j + 1, :]
        weight = 1.0 / jnp.sqrt(pivots)
        left = left * weight
        right = right * weight
        out[here, :rank] = left
        out[here, rank:] = right
        if start + PANEL < rank:
            rows = jnp.concatenate([left, right], 1)
            high, rest = split(rows)
            middle = rest
            low = (rows - high.astype(jnp.float32) - middle.astype(jnp.float32)).astype(jnp.bfloat16)
            one = jnp.concatenate([high, high, middle, middle, high, low], 0)[:, :rank]
            two = jnp.concatenate([high, middle, high, middle, low, high], 0)
            update = dot(one, two, 0, 0)
            below = slice(start + PANEL, rank)
            out[below, :] = out[below, :] - update[start + PANEL :, :]


def factor(panels, rank, inputs, grams, block):
    return pl.pallas_call(
        functools.partial(factor_kernel, panels, grams, block),
        in_specs=[VMEM] * len(inputs),
        out_specs=VMEM,
        out_shape=pltpu.VMEM((rank, 2 * rank), jnp.float32),
        compiler_params=params(16),
        name="factor",
    )(*inputs)


LOADS = 4


def load_kernel(source, token, held, sem):
    rows = source.shape[0] // LOADS
    copies = []
    for n in range(LOADS):
        here = pl.ds(n * rows, rows)
        copies.append(pltpu.make_async_copy(source.at[here], held.at[here], sem.at[n]))
        copies[-1].start()
    for copy in copies:
        copy.wait()


def load(source, token):
    return pl.pallas_call(
        load_kernel,
        in_specs=[ANY, ANY],
        out_specs=VMEM,
        out_shape=pltpu.VMEM(source.shape, source.dtype),
        scratch_shapes=[pltpu.SemaphoreType.DMA((LOADS,))],
        compiler_params=params(FIRST_MIB),
        name="load",
    )(source, token)


def ortho_kernel(group, who, state, *refs):
    sketches, refs = refs[: PARTS * group], refs[PARTS * group :]
    ortho, own_ortho, total = refs
    rank = state.shape[0]
    part = sketches[0].shape[0]
    inverse = state[:, rank:]
    for s in range(group):
        for p in range(PARTS):
            value = sketches[s * PARTS + p][...]
            high, low = split(value)
            first, second = split(inverse)
            wide = dot(high, jnp.concatenate([first, second], 0), 1, 1)
            value = wide[:, :rank] + wide[:, rank:] + dot(low, first, 1, 1)
            rows = slice((s * PARTS + p) * part, (s * PARTS + p + 1) * part)
            ortho[rows, :] = jnp.concatenate(split(value), 1)
            start = ((who[0] ^ s) * PARTS + p) * part
            total[pl.ds(pl.multiple_of(start, part), part), :] = value
    own = own_ortho.shape[0]
    own_ortho[...] = total[pl.ds(pl.multiple_of(who[1] * own, own), own), :]


def orthonormal(who, state, sketches, group, n_dp):
    rank = state.shape[0]
    rows = sketches[0].shape[0] * len(sketches)
    return pl.pallas_call(
        functools.partial(ortho_kernel, group),
        in_specs=[SMEM] + [VMEM] * (1 + len(sketches)),
        out_specs=[VMEM] * 2,
        out_shape=[
            pltpu.VMEM((rows, 2 * rank), jnp.bfloat16),
            pltpu.VMEM((rows // n_dp, rank), jnp.float32),
        ],
        scratch_shapes=[pltpu.VMEM((rows, rank), jnp.float32)],
        compiler_params=params(16),
        name="ortho",
    )(who, state, *sketches)


CUTS = 2


def finish_kernel(group, places, scale, who, right_here, right_there, state, ortho, own_ortho, *refs):
    blended, new_momentum, new_basis, update, right, values, coeff_high, coeff_low, basis_held, update_held, sem = refs
    rank, kv = right.shape
    half = rank // 2
    core = who[2] & 1
    right[pl.ds(pl.multiple_of(core * half, half), half), :] = right_here[...]
    right[pl.ds(pl.multiple_of((1 - core) * half, half), half), :] = right_there[...]
    coeff = dot(state[:, rank:], right[...], 1, 0, EXACT)
    high, low = split(0.2 * coeff)
    coeff_high[:rank, :] = high
    coeff_high[rank:, :] = high
    coeff_low[...] = low
    block = values.shape[0] // group
    rows = block // CUTS
    copies = []
    for s in range(group):
        for c in range(CUTS):
            here = slice(s * block + c * rows, s * block + (c + 1) * rows)
            part = ortho[here, :]
            feedback = dot(part, coeff_high[...], 1, 0) + dot(part[:, :rank], coeff_low[...], 1, 0)
            at = places[s] + c * rows
            values[here, :] = blended[at : at + rows, :] - feedback
            there = pl.multiple_of((who[0] ^ s) * block + c * rows, rows)
            copies.append(
                pltpu.make_async_copy(values.at[here], new_momentum.at[pl.ds(there, rows)], sem.at[len(copies)])
            )
            copies[-1].start()
    norm = jnp.sqrt(jnp.sum(coeff * coeff, axis=1, keepdims=True) + 1e-06)
    normed = coeff / norm
    count = new_basis.shape[0]
    for j in range(kv // count):

        @pl.when(who[2] == j)
        def _(j=j):
            basis_held[...] = normed[:, j * count : (j + 1) * count].T

    copies.append(pltpu.make_async_copy(basis_held, new_basis, sem.at[len(copies)]))
    copies[-1].start()
    rows_high, rows_low = split(own_ortho[...])
    high, low = split(normed)
    product = dot(jnp.concatenate([rows_high, rows_low], 1), jnp.concatenate([high, high], 0), 1, 0)
    update_held[...] = (scale * (product + dot(rows_high, low, 1, 0))).astype(update.dtype)
    copies.append(pltpu.make_async_copy(update_held, update, sem.at[len(copies)]))
    copies[-1].start()
    for copy in copies:
        copy.wait()


def finish(who, right_here, right_there, state, ortho, own_ortho, blended, places, n_rows, scale):
    rank, kv = 2 * right_here.shape[0], right_here.shape[1]
    group = len(places)
    rows = ortho.shape[0]
    return pl.pallas_call(
        functools.partial(finish_kernel, group, places, scale),
        in_specs=[SMEM] + [VMEM] * 6,
        out_specs=[ANY, ANY, ANY],
        out_shape=[
            jax.ShapeDtypeStruct((rows, kv), jnp.float32),
            jax.ShapeDtypeStruct((kv // n_rows, rank), jnp.float32),
            jax.ShapeDtypeStruct(own_ortho.shape[:1] + (kv,), jnp.bfloat16),
        ],
        scratch_shapes=[
            pltpu.VMEM((rank, kv), jnp.float32),
            pltpu.VMEM((rows, kv), jnp.float32),
            pltpu.VMEM((2 * rank, kv), jnp.bfloat16),
            pltpu.VMEM((rank, kv), jnp.bfloat16),
            pltpu.VMEM((kv // n_rows, rank), jnp.float32),
            pltpu.VMEM(own_ortho.shape[:1] + (kv,), jnp.bfloat16),
            pltpu.SemaphoreType.DMA((group * CUTS + 2,)),
        ],
        compiler_params=params(32),
        name="finish",
    )(who, right_here, right_there, state, ortho, own_ortho, blended)


def body(activations, key_grads, momentum, basis):
    n_dp = lax.axis_size("dp")
    n_rows = lax.axis_size("rows")
    dp = lax.axis_index("dp")
    group = min(4, n_dp)
    low = dp & (group - 1)
    kv, rank = basis.shape
    local_rows = activations.shape[1]
    block = local_rows // group
    part = block // PARTS
    far = [mask for mask in bits_of(n_dp) if mask >= group]
    plane = [("rows", m) for m in bits_of(n_rows)[1:]] + [("dp", 1)]
    mine = sum(bit_set(a, m) << b for b, (a, m) in enumerate(plane))
    who = jnp.stack([low, dp, lax.axis_index("rows"), mine]).astype(jnp.int32)

    offsets, later = tuple(range(group - 1, 1, -1)), (1, 0)
    blended, held, acts_later, momentum_later, given = first_blend(
        activations, key_grads, momentum[0], basis, group, offsets, later
    )
    places = [0] * group
    arrived = [[] for _ in range(PARTS)]
    for i, offset in enumerate(offsets):
        places[offset] = i * block
        for p in range(PARTS):
            arrived[p].append(swap(given[i * PARTS + p], {"dp": offset}))
    for n, offset in enumerate(later):
        places[offset] = (len(offsets) + n) * block
    own = [None] * PARTS
    for calls in CALLS:
        jobs = tuple((n, p, places[later[n]]) for n, p in calls)
        blended, given = blend(acts_later, held, basis, momentum_later, blended, jobs)
        for (n, p), value in zip(calls, given):
            if later[n] == 0:
                own[p] = value
            else:
                arrived[p].append(swap(value, {"dp": later[n]}))
    sketches = [[None] * PARTS for _ in range(group)]
    for p in range(PARTS):
        for piece in arrived[p]:
            own[p] = own[p] + piece
        for mask in far:
            own[p] = own[p] + swap(own[p], {"dp": mask})
        own[p] = own[p] * (1.0 / n_dp)
        sketches[0][p] = own[p]
        for s in range(group - 1, 0, -1):
            sketches[s][p] = swap(own[p], {"dp": s})

    scale = 1.0 / n_dp
    pieces = [(places[0] + p * part, part) for p in range(PARTS)]
    *befores, held = right_terms(who, blended, pieces, own, scale, first=True)
    for p in range(PARTS):
        pieces = [(places[s] + p * part, part) for s in range(1, group)]
        given = [sketches[s][p] for s in range(1, group)]
        if p + 1 < PARTS:
            befores += right_terms(who, held, pieces, given, scale)
        else:
            keep, give = right_terms(who, held, pieces, given, scale, befores)

    count = 1 << len(plane)
    *blocks, gram = cut(who, keep, swap(give, {"rows": 1}), rank, count)
    right = blocks[0]
    block = right.shape[0]
    grams = [gram]
    for s in range(count - 1, 0, -1):
        piece = swap(blocks[s], masks_of([d for b, d in enumerate(plane) if s >> b & 1]))
        if s < count // 2:
            grams.append(piece)
            piece = piece[:block]
        right = right + piece
    panels = list(range(0, rank, PANEL))
    middle = len(panels) // 2
    state = factor(panels, rank, grams, len(grams), block)
    masks = bits_of(n_dp)[1:]
    for first in range(0, len(masks), 2):
        pair = masks[first : first + 2]
        pieces = [swap(right, {"dp": mask}) for mask in ([sum(pair)] + pair[::-1])[: 2 ** len(pair) - 1]]
        *pieces, state = lax.optimization_barrier((*pieces, state))
        for piece in pieces:
            right = right + piece
    flat = [sketches[s][p] for s in range(group) for p in range(PARTS)]
    right, held = gather(right, plane, load(blended, right))
    other = swap(right, {"rows": 1})
    ortho, own_ortho = orthonormal(who, state, flat, group, n_dp)

    new_momentum, new_basis, update = finish(
        who, right, other, state, ortho, own_ortho, held, places, n_rows,
        math.sqrt(local_rows * n_rows * kv / rank),
    )
    return (new_momentum[None], new_basis, update)


def solution(mesh):
    in_specs = (P("dp", "rows"), P("dp", None), P("dp", "rows", None), P())
    out_specs = (P("dp", "rows", None), P("rows", None), P(("rows", "dp"), None))
    return jax.shard_map(body, mesh=mesh, in_specs=in_specs, out_specs=out_specs, check_vma=False)
```

```python
import functools
import math

import jax
import jax.numpy as jnp
from jax import lax
from jax.experimental import pallas as pl
from jax.experimental.pallas import tpu as pltpu
from jax.sharding import PartitionSpec as P

MIB = 1024 * 1024
FIRST_MIB = 44
BLEND_MIB = 40
EXACT = lax.Precision.HIGHEST


def split(value):
    high = value.astype(jnp.bfloat16)
    return high, (value - high.astype(jnp.float32)).astype(jnp.bfloat16)


def dot(left, right, left_dim, right_dim, precision=None):
    return lax.dot_general(
        left,
        right,
        (((left_dim,), (right_dim,)), ((), ())),
        precision=precision,
        preferred_element_type=jnp.float32,
    )


def params(mib):
    return pltpu.CompilerParams(vmem_limit_bytes=mib * MIB)


def swap(value, masks):
    axes = tuple(a for a in ("dp", "rows") if a in masks)
    sizes = [lax.axis_size(a) for a in axes]
    pairs = []
    for index in range(math.prod(sizes)):
        rest, there = index, 0
        coords = []
        for size in sizes[::-1]:
            coords.append(rest % size)
            rest //= size
        for axis, size, coord in zip(axes, sizes, coords[::-1]):
            there = there * size + (coord ^ masks[axis])
        pairs.append((index, there))
    return lax.ppermute(value, axes, pairs)


def bits_of(count):
    return [1 << b for b in range(count.bit_length() - 1)]


def bit_set(axis, mask):
    return jnp.where((lax.axis_index(axis) & mask) != 0, 1, 0).astype(jnp.int32)


def masks_of(chosen):
    masks = {}
    for axis, mask in chosen:
        masks[axis] = masks.get(axis, 0) | mask
    return masks


def gather(value, directions, beside):
    count = 1 << len(directions)
    block = value.shape[0]
    mine = sum(bit_set(a, m) << b for b, (a, m) in enumerate(directions))
    parts = [value] + [
        swap(value, masks_of([d for b, d in enumerate(directions) if s >> b & 1])) for s in range(1, count)
    ]
    *parts, beside = lax.optimization_barrier((*parts, beside))
    out = jnp.zeros((count * block,) + value.shape[1:], value.dtype)
    for s, part in enumerate(parts):
        out = lax.dynamic_update_slice_in_dim(out, part, (mine ^ s) * block, 0)
    return out, beside


VMEM = pl.BlockSpec(memory_space=pltpu.VMEM)
ANY = pl.BlockSpec(memory_space=pl.ANY)
SMEM = pl.BlockSpec(memory_space=pltpu.SMEM)
PARTS = 2
CALLS = (((0, 0), (0, 1)), ((1, 0), (1, 1)))


def sketch_of(value, both, rank):
    high, low = split(value)
    wide = dot(high, both, 1, 0)
    return wide[:, :rank] + wide[:, rank:] + dot(low, both[:, :rank], 1, 0)


CHUNKS = 2


def first_blend_kernel(group, offsets, later, acts, grads, momentum, basis, *refs):
    count, extra = len(offsets), len(later)
    blended, held, acts_later = refs[:3]
    momentum_later = refs[3 : 3 + extra]
    sketches = refs[3 + extra : 3 + extra + PARTS * count]
    refs = refs[3 + extra + PARTS * count :]
    acts_held, values, basis_held, both, acts_sem, grads_sem, momentum_sem, later_sem, out_sem, basis_sem = refs
    low = lax.axis_index("dp") & (group - 1)
    tokens, block = acts_held.shape[1:]
    rank = basis.shape[1]
    chunk = tokens // CHUNKS
    part = block // PARTS

    def start_of(offset):
        return pl.multiple_of((low ^ offset) * block, block)

    def acts_copy(i, c):
        here = pl.ds(c * chunk, chunk)
        return pltpu.make_async_copy(
            acts.at[here, pl.ds(start_of(offsets[i]), block)], acts_held.at[i, here], acts_sem.at[i, c]
        )

    def grads_copy(c):
        here = pl.ds(c * chunk, chunk)
        return pltpu.make_async_copy(grads.at[here], held.at[here], grads_sem.at[c])

    def momentum_copy(i):
        return pltpu.make_async_copy(
            momentum.at[pl.ds(start_of(offsets[i]), block)],
            values.at[pl.ds(i * block, block)],
            momentum_sem.at[i],
        )

    def out_copy(index):
        here = pl.ds(index * part, part)
        return pltpu.make_async_copy(values.at[here], blended.at[here], out_sem.at[index])

    def later_copies(i):
        here = pl.ds(start_of(later[i]), block)
        return [
            pltpu.make_async_copy(acts.at[:, here], acts_later.at[i], later_sem.at[i, 0]),
            pltpu.make_async_copy(momentum.at[here], momentum_later[i], later_sem.at[i, 1]),
        ]

    for c in range(CHUNKS):
        acts_copy(0, c).start()
        grads_copy(c).start()
    basis_copy = pltpu.make_async_copy(basis, basis_held, basis_sem)
    basis_copy.start()
    columns = [slice(p * part, (p + 1) * part) for p in range(PARTS)]
    for i in range(count):
        if i == 0:
            sums = None
            for c in range(CHUNKS):
                acts_copy(0, c).wait()
                grads_copy(c).wait()
                if c == CHUNKS // 2:
                    momentum_copy(0).start()
                here = slice(c * chunk, (c + 1) * chunk)
                terms = [dot(acts_held[0, here, cols], held[here, :], 0, 0) for cols in columns]
                sums = terms if c == 0 else [a + b for a, b in zip(sums, terms)]
        else:
            for c in range(CHUNKS):
                acts_copy(i, c).wait()
        if i + 1 < count:
            for c in range(CHUNKS):
                acts_copy(i + 1, c).start()
            momentum_copy(i + 1).start()
        else:
            for n in range(extra):
                for copy in later_copies(n):
                    copy.start()
        momentum_copy(i).wait()
        for p, cols in enumerate(columns):
            rows = slice(i * block + p * part, i * block + (p + 1) * part)
            gradient = sums[p] if i == 0 else dot(acts_held[i, :, cols], held[...], 0, 0)
            values[rows, :] = values[rows, :] + gradient
            out_copy(i * PARTS + p).start()
        if i == 0:
            basis_copy.wait()
            basis_high, basis_low = split(basis_held[...])
            both[:, :rank] = basis_high
            both[:, rank:] = basis_low
        for index in range(i * PARTS, (i + 1) * PARTS):
            sketches[index][...] = sketch_of(values[index * part : (index + 1) * part, :], both[...], rank)
    for index in range(count * PARTS):
        out_copy(index).wait()
    for n in range(extra):
        for copy in later_copies(n):
            copy.wait()


def first_blend(acts, grads, momentum, basis, group, offsets, later):
    tokens, rows = acts.shape
    kv, rank = basis.shape
    block = rows // group
    count, extra = len(offsets), len(later)
    outs = [
        jax.ShapeDtypeStruct((rows, kv), jnp.float32),
        pltpu.VMEM((tokens, kv), jnp.bfloat16),
        pltpu.VMEM((extra, tokens, block), jnp.bfloat16),
    ]
    outs += [pltpu.VMEM((block, kv), jnp.float32)] * extra
    outs += [pltpu.VMEM((block // PARTS, rank), jnp.float32)] * (PARTS * count)
    out = pl.pallas_call(
        functools.partial(first_blend_kernel, group, offsets, later),
        in_specs=[ANY, ANY, ANY, ANY],
        out_specs=[ANY] + [VMEM] * (len(outs) - 1),
        out_shape=outs,
        scratch_shapes=[
            pltpu.VMEM((count, tokens, block), jnp.bfloat16),
            pltpu.VMEM((count * block, kv), jnp.float32),
            pltpu.VMEM((kv, rank), jnp.float32),
            pltpu.VMEM((kv, 2 * rank), jnp.bfloat16),
            pltpu.SemaphoreType.DMA((count, CHUNKS)),
            pltpu.SemaphoreType.DMA((CHUNKS,)),
            pltpu.SemaphoreType.DMA((count,)),
            pltpu.SemaphoreType.DMA((extra, 2)),
            pltpu.SemaphoreType.DMA((count * PARTS,)),
            pltpu.SemaphoreType.DMA,
        ],
        compiler_params=params(FIRST_MIB),
        name="first_blend",
    )(acts, grads, momentum, basis)
    return out[0], out[1], out[2], out[3 : 3 + extra], out[3 + extra :]


def blend_kernel(jobs, extra, acts, grads, basis, *refs):
    momentum, refs = refs[:extra], refs[extra + 1 :]
    blended, sketches, (values, out_sem) = refs[0], refs[1:-2], refs[-2:]
    rank = basis.shape[1]
    part = values.shape[0] // len(jobs)
    both = jnp.concatenate(split(basis[...]), 1)
    copies = []
    for n, (which, p, place) in enumerate(jobs):
        here = slice(n * part, (n + 1) * part)
        rows = slice(p * part, (p + 1) * part)
        values[here, :] = momentum[which][rows, :] + dot(acts[which, :, rows], grads[...], 0, 0)
        copies.append(
            pltpu.make_async_copy(values.at[here], blended.at[pl.ds(place + p * part, part)], out_sem.at[n])
        )
        copies[-1].start()
    for n, sketch in enumerate(sketches):
        sketch[...] = sketch_of(values[n * part : (n + 1) * part, :], both, rank)
    for copy in copies:
        copy.wait()


def blend(acts, grads, basis, momentum, blended, jobs):
    block = acts.shape[2]
    kv, rank = basis.shape
    part = block // PARTS
    outs = [jax.ShapeDtypeStruct(blended.shape, jnp.float32)]
    outs += [pltpu.VMEM((part, rank), jnp.float32)] * len(jobs)
    out = pl.pallas_call(
        functools.partial(blend_kernel, jobs, len(momentum)),
        in_specs=[VMEM] * (3 + len(momentum)) + [ANY],
        out_specs=[ANY] + [VMEM] * len(jobs),
        out_shape=outs,
        scratch_shapes=[
            pltpu.VMEM((len(jobs) * part, kv), jnp.float32),
            pltpu.SemaphoreType.DMA((len(jobs),)),
        ],
        input_output_aliases={3 + len(momentum): 0},
        compiler_params=params(BLEND_MIB),
        name="blend",
    )(acts, grads, basis, *momentum, blended)
    return out[0], out[1:]


def right_product(sketch, blended):
    turned = sketch.T
    rank = turned.shape[0]
    high, low = split(turned)
    stacked = jnp.concatenate([high, low], 0)
    blended_high, blended_low = split(blended)
    wide = dot(stacked, blended_high, 1, 0)
    gram = dot(stacked, stacked, 1, 1)
    gram = gram[:rank, :rank] + gram[rank:, rank:] + (gram[:rank, rank:] + gram[rank:, :rank])
    return wide[:rank] + wide[rank:] + dot(high, blended_low, 1, 0), gram


def pack(gram, width):
    rank = gram.shape[0]
    rows = rank * rank // width
    return jnp.concatenate([gram[k * rows : (k + 1) * rows, :] for k in range(rank // rows)], 1)


def unpack(packed, rank):
    return jnp.concatenate([packed[:, k * rank : (k + 1) * rank] for k in range(packed.shape[1] // rank)], 0)


def right_kernel(pieces, first, last, scale, *refs):
    who, blended = refs[:2]
    refs = refs[2:]
    sketches, refs = refs[: len(pieces)], refs[len(pieces) :]
    if first:
        held, sem = refs[-2:]
        start, rows = pieces[0][0], sum(r for _, r in pieces)
        copies = []
        for at, size in ((start, rows), (0, start), (start + rows, blended.shape[0] - start - rows)):
            if size:
                here = pl.ds(at, size)
                copies.append(pltpu.make_async_copy(blended.at[here], held.at[here], sem.at[len(copies)]))
                copies[-1].start()
        copies[0].wait()
        blended = held
    right, gram = None, None
    for (start, rows), sketch in zip(pieces, sketches):
        right_term, gram_term = right_product(sketch[...], blended[start : start + rows, :])
        right = right_term if right is None else right + right_term
        gram = gram_term if gram is None else gram + gram_term
    right = scale * right
    if not last:
        refs[0][...] = right
        refs[1][...] = gram
        if first:
            for copy in copies[1:]:
                copy.wait()
        return
    befores, refs = refs[:-3], refs[-3:]
    keep, give, total = refs
    for before in befores[::2]:
        right = right + before[...]
    for before in befores[1::2]:
        gram = gram + before[...]
    total[...] = right
    half = total.shape[0] // 2
    core = who[2] & 1
    keep[:half, :] = total[pl.ds(pl.multiple_of(core * half, half), half), :]
    give[:half, :] = total[pl.ds(pl.multiple_of((1 - core) * half, half), half), :]
    packed = pack(gram, right.shape[1])
    keep[half:, :] = packed
    give[half:, :] = packed


def right_terms(who, blended, pieces, sketches, scale, befores=None, first=False):
    rank = sketches[0].shape[1]
    kv = blended.shape[1]
    last = befores is not None
    gram = pltpu.VMEM((rank, rank), jnp.float32)
    if last:
        outs = [pltpu.VMEM((rank // 2 + rank * rank // kv, kv), jnp.float32)] * 2
    else:
        outs = [pltpu.VMEM((rank, kv), jnp.float32), pltpu.VMEM((rank, rank), jnp.float32)]
    scratch = [pltpu.VMEM((rank, kv), jnp.float32)] if last else []
    if first:
        outs.append(pltpu.VMEM(blended.shape, jnp.float32))
        scratch = [pltpu.SemaphoreType.DMA((3,))]
    operands = [who, blended, *sketches, *(befores or [])]
    return pl.pallas_call(
        functools.partial(right_kernel, pieces, first, last, scale),
        in_specs=[SMEM, ANY if first else VMEM] + [VMEM] * (len(operands) - 2),
        out_specs=[VMEM] * len(outs),
        out_shape=outs,
        scratch_shapes=scratch,
        compiler_params=params(FIRST_MIB if first else 16),
        name="right_terms",
    )(*operands)


def cut_kernel(count, who, keep, arrived, *outs):
    blocks, gram = outs[:-1], outs[-1]
    block = blocks[0].shape[0]
    half = count * block
    packed = keep[half:, :] + arrived[half:, :]
    gram[...] = packed
    for s, out in enumerate(blocks):
        here = pl.ds(pl.multiple_of((who[3] ^ s) * block, block), block)
        out[:block, :] = keep[here, :] + arrived[here, :]
        if 0 < s < count // 2:
            out[block:, :] = packed


def cut(who, keep, arrived, rank, count):
    kv = keep.shape[1]
    block = rank // 2 // count
    extra = rank * rank // kv
    shapes = [(block + (extra if 0 < s < count // 2 else 0), kv) for s in range(count)] + [(extra, kv)]
    return pl.pallas_call(
        functools.partial(cut_kernel, count),
        in_specs=[SMEM, VMEM, VMEM],
        out_specs=[VMEM] * len(shapes),
        out_shape=[pltpu.VMEM(shape, jnp.float32) for shape in shapes],
        compiler_params=params(16),
        name="cut",
    )(who, keep, arrived)


PANEL = 16


def factor_kernel(panels, grams, block, *refs):
    out = refs[-1]
    rank = out.shape[0]
    if grams:
        packed = refs[0][...]
        for ref in refs[1:grams]:
            packed = packed + ref[block:, :]
        rows_id = lax.broadcasted_iota(jnp.int32, (rank, rank), 0)
        cols_id = lax.broadcasted_iota(jnp.int32, (rank, rank), 1)
        out[:, :rank] = unpack(packed, rank)
        out[:, rank:] = jnp.where(rows_id == cols_id, 1.0, 0.0)
    else:
        out[...] = refs[0][...]
    index = lax.broadcasted_iota(jnp.int32, (PANEL, rank), 0)
    for start in panels:
        here = slice(start, start + PANEL)
        left = out[here, :rank]
        right = out[here, rank:]
        columns = [
            jnp.broadcast_to(left[:, start + c : start + c + 1], (PANEL, rank)) for c in range(PANEL)
        ]
        pivots = jnp.ones((PANEL, rank), jnp.float32)
        for j in range(PANEL):
            pivot = columns[j][j : j + 1, :]
            pivots = jnp.where(index == j, pivot, pivots)
            factor = jnp.where(index > j, columns[j] * (1.0 / pivot), 0.0)
            for c in range(j + 1, PANEL):
                columns[c] = columns[c] - factor * columns[c][j : j + 1, :]
            left = left - factor * left[j : j + 1, :]
            right = right - factor * right[j : j + 1, :]
        weight = 1.0 / jnp.sqrt(pivots)
        left = left * weight
        right = right * weight
        out[here, :rank] = left
        out[here, rank:] = right
        if start + PANEL < rank:
            rows = jnp.concatenate([left, right], 1)
            high, rest = split(rows)
            middle = rest
            low = (rows - high.astype(jnp.float32) - middle.astype(jnp.float32)).astype(jnp.bfloat16)
            one = jnp.concatenate([high, high, middle, middle, high, low], 0)[:, :rank]
            two = jnp.concatenate([high, middle, high, middle, low, high], 0)
            update = dot(one, two, 0, 0)
            below = slice(start + PANEL, rank)
            out[below, :] = out[below, :] - update[start + PANEL :, :]


def factor(panels, rank, inputs, grams, block):
    return pl.pallas_call(
        functools.partial(factor_kernel, panels, grams, block),
        in_specs=[VMEM] * len(inputs),
        out_specs=VMEM,
        out_shape=pltpu.VMEM((rank, 2 * rank), jnp.float32),
        compiler_params=params(16),
        name="factor",
    )(*inputs)


LOADS = 4


def load_kernel(source, token, held, sem):
    rows = source.shape[0] // LOADS
    copies = []
    for n in range(LOADS):
        here = pl.ds(n * rows, rows)
        copies.append(pltpu.make_async_copy(source.at[here], held.at[here], sem.at[n]))
        copies[-1].start()
    for copy in copies:
        copy.wait()


def load(source, token):
    return pl.pallas_call(
        load_kernel,
        in_specs=[ANY, ANY],
        out_specs=VMEM,
        out_shape=pltpu.VMEM(source.shape, source.dtype),
        scratch_shapes=[pltpu.SemaphoreType.DMA((LOADS,))],
        compiler_params=params(FIRST_MIB),
        name="load",
    )(source, token)


def ortho_kernel(group, who, state, *refs):
    sketches, refs = refs[: PARTS * group], refs[PARTS * group :]
    ortho, own_ortho, total = refs
    rank = state.shape[0]
    part = sketches[0].shape[0]
    inverse = state[:, rank:]
    for s in range(group):
        for p in range(PARTS):
            value = sketches[s * PARTS + p][...]
            high, low = split(value)
            first, second = split(inverse)
            wide = dot(high, jnp.concatenate([first, second], 0), 1, 1)
            value = wide[:, :rank] + wide[:, rank:] + dot(low, first, 1, 1)
            rows = slice((s * PARTS + p) * part, (s * PARTS + p + 1) * part)
            high, low = split(0.2 * value)
            wide = dot(high, jnp.concatenate([first, second], 1), 1, 0)
            turned = wide[:, :rank] + wide[:, rank:] + dot(low, first, 1, 0)
            ortho[rows, :] = jnp.concatenate(split(turned), 1)
            start = ((who[0] ^ s) * PARTS + p) * part
            total[pl.ds(pl.multiple_of(start, part), part), :] = value
    own = own_ortho.shape[0]
    own_ortho[...] = total[pl.ds(pl.multiple_of(who[1] * own, own), own), :]


def orthonormal(who, state, sketches, group, n_dp):
    rank = state.shape[0]
    rows = sketches[0].shape[0] * len(sketches)
    return pl.pallas_call(
        functools.partial(ortho_kernel, group),
        in_specs=[SMEM] + [VMEM] * (1 + len(sketches)),
        out_specs=[VMEM] * 2,
        out_shape=[
            pltpu.VMEM((rows, 2 * rank), jnp.bfloat16),
            pltpu.VMEM((rows // n_dp, rank), jnp.float32),
        ],
        scratch_shapes=[pltpu.VMEM((rows, rank), jnp.float32)],
        compiler_params=params(16),
        name="ortho",
    )(who, state, *sketches)


CUTS = 2


def finish_kernel(group, places, scale, who, right_here, right_there, state, ortho, own_ortho, *refs):
    blended, new_momentum, new_basis, update, right, values, right_high, right_low, basis_held, update_held, sem = refs
    rank, kv = right.shape
    half = rank // 2
    core = who[2] & 1
    right[pl.ds(pl.multiple_of(core * half, half), half), :] = right_here[...]
    right[pl.ds(pl.multiple_of((1 - core) * half, half), half), :] = right_there[...]
    high, low = split(right[...])
    right_high[:rank, :] = high
    right_high[rank:, :] = high
    right_low[...] = low
    block = values.shape[0] // group
    rows = block // CUTS
    copies = []
    for s in range(group):
        for c in range(CUTS):
            here = slice(s * block + c * rows, s * block + (c + 1) * rows)
            part = ortho[here, :]
            feedback = dot(part, right_high[...], 1, 0) + dot(part[:, :rank], right_low[...], 1, 0)
            at = places[s] + c * rows
            values[here, :] = blended[at : at + rows, :] - feedback
            there = pl.multiple_of((who[0] ^ s) * block + c * rows, rows)
            copies.append(
                pltpu.make_async_copy(values.at[here], new_momentum.at[pl.ds(there, rows)], sem.at[len(copies)])
            )
            copies[-1].start()
    coeff = dot(state[:, rank:], right[...], 1, 0, EXACT)
    norm = jnp.sqrt(jnp.sum(coeff * coeff, axis=1, keepdims=True) + 1e-06)
    normed = coeff / norm
    count = new_basis.shape[0]
    for j in range(kv // count):

        @pl.when(who[2] == j)
        def _(j=j):
            basis_held[...] = normed[:, j * count : (j + 1) * count].T

    copies.append(pltpu.make_async_copy(basis_held, new_basis, sem.at[len(copies)]))
    copies[-1].start()
    rows_high, rows_low = split(own_ortho[...])
    high, low = split(normed)
    product = dot(jnp.concatenate([rows_high, rows_low], 1), jnp.concatenate([high, high], 0), 1, 0)
    update_held[...] = (scale * (product + dot(rows_high, low, 1, 0))).astype(update.dtype)
    copies.append(pltpu.make_async_copy(update_held, update, sem.at[len(copies)]))
    copies[-1].start()
    for copy in copies:
        copy.wait()


def finish(who, right_here, right_there, state, ortho, own_ortho, blended, places, n_rows, scale):
    rank, kv = 2 * right_here.shape[0], right_here.shape[1]
    group = len(places)
    rows = ortho.shape[0]
    return pl.pallas_call(
        functools.partial(finish_kernel, group, places, scale),
        in_specs=[SMEM] + [VMEM] * 6,
        out_specs=[ANY, ANY, ANY],
        out_shape=[
            jax.ShapeDtypeStruct((rows, kv), jnp.float32),
            jax.ShapeDtypeStruct((kv // n_rows, rank), jnp.float32),
            jax.ShapeDtypeStruct(own_ortho.shape[:1] + (kv,), jnp.bfloat16),
        ],
        scratch_shapes=[
            pltpu.VMEM((rank, kv), jnp.float32),
            pltpu.VMEM((rows, kv), jnp.float32),
            pltpu.VMEM((2 * rank, kv), jnp.bfloat16),
            pltpu.VMEM((rank, kv), jnp.bfloat16),
            pltpu.VMEM((kv // n_rows, rank), jnp.float32),
            pltpu.VMEM(own_ortho.shape[:1] + (kv,), jnp.bfloat16),
            pltpu.SemaphoreType.DMA((group * CUTS + 2,)),
        ],
        compiler_params=params(32),
        name="finish",
    )(who, right_here, right_there, state, ortho, own_ortho, blended)


def body(activations, key_grads, momentum, basis):
    n_dp = lax.axis_size("dp")
    n_rows = lax.axis_size("rows")
    dp = lax.axis_index("dp")
    group = min(4, n_dp)
    low = dp & (group - 1)
    kv, rank = basis.shape
    local_rows = activations.shape[1]
    block = local_rows // group
    part = block // PARTS
    far = [mask for mask in bits_of(n_dp) if mask >= group]
    plane = [("rows", m) for m in bits_of(n_rows)[1:]] + [("dp", 1)]
    mine = sum(bit_set(a, m) << b for b, (a, m) in enumerate(plane))
    who = jnp.stack([low, dp, lax.axis_index("rows"), mine]).astype(jnp.int32)

    offsets, later = tuple(range(group - 1, 1, -1)), (1, 0)
    blended, held, acts_later, momentum_later, given = first_blend(
        activations, key_grads, momentum[0], basis, group, offsets, later
    )
    places = [0] * group
    arrived = [[] for _ in range(PARTS)]
    for i, offset in enumerate(offsets):
        places[offset] = i * block
        for p in range(PARTS):
            arrived[p].append(swap(given[i * PARTS + p], {"dp": offset}))
    for n, offset in enumerate(later):
        places[offset] = (len(offsets) + n) * block
    own = [None] * PARTS
    for calls in CALLS:
        jobs = tuple((n, p, places[later[n]]) for n, p in calls)
        blended, given = blend(acts_later, held, basis, momentum_later, blended, jobs)
        for (n, p), value in zip(calls, given):
            if later[n] == 0:
                own[p] = value
            else:
                arrived[p].append(swap(value, {"dp": later[n]}))
    sketches = [[None] * PARTS for _ in range(group)]
    for p in range(PARTS):
        for piece in arrived[p]:
            own[p] = own[p] + piece
        for mask in far:
            own[p] = own[p] + swap(own[p], {"dp": mask})
        own[p] = own[p] * (1.0 / n_dp)
        sketches[0][p] = own[p]
        for s in range(group - 1, 0, -1):
            sketches[s][p] = swap(own[p], {"dp": s})

    scale = 1.0 / n_dp
    pieces = [(places[0] + p * part, part) for p in range(PARTS)]
    *befores, held = right_terms(who, blended, pieces, own, scale, first=True)
    for p in range(PARTS):
        pieces = [(places[s] + p * part, part) for s in range(1, group)]
        given = [sketches[s][p] for s in range(1, group)]
        if p + 1 < PARTS:
            befores += right_terms(who, held, pieces, given, scale)
        else:
            keep, give = right_terms(who, held, pieces, given, scale, befores)

    count = 1 << len(plane)
    *blocks, gram = cut(who, keep, swap(give, {"rows": 1}), rank, count)
    right = blocks[0]
    block = right.shape[0]
    grams = [gram]
    for s in range(count - 1, 0, -1):
        piece = swap(blocks[s], masks_of([d for b, d in enumerate(plane) if s >> b & 1]))
        if s < count // 2:
            grams.append(piece)
            piece = piece[:block]
        right = right + piece
    panels = list(range(0, rank, PANEL))
    middle = len(panels) // 2
    state = factor(panels, rank, grams, len(grams), block)
    masks = bits_of(n_dp)[1:]
    for first in range(0, len(masks), 2):
        pair = masks[first : first + 2]
        pieces = [swap(right, {"dp": mask}) for mask in ([sum(pair)] + pair[::-1])[: 2 ** len(pair) - 1]]
        *pieces, state = lax.optimization_barrier((*pieces, state))
        for piece in pieces:
            right = right + piece
    flat = [sketches[s][p] for s in range(group) for p in range(PARTS)]
    right, held = gather(right, plane, load(blended, right))
    other = swap(right, {"rows": 1})
    ortho, own_ortho = orthonormal(who, state, flat, group, n_dp)

    new_momentum, new_basis, update = finish(
        who, right, other, state, ortho, own_ortho, held, places, n_rows,
        math.sqrt(local_rows * n_rows * kv / rank),
    )
    return (new_momentum[None], new_basis, update)


def solution(mesh):
    in_specs = (P("dp", "rows"), P("dp", None), P("dp", "rows", None), P())
    out_specs = (P("dp", "rows", None), P("rows", None), P(("rows", "dp"), None))
    return jax.shard_map(body, mesh=mesh, in_specs=in_specs, out_specs=out_specs, check_vma=False)
```
